32 devices in a mesh: groups: 2 (over y), cls: 4 (over z), img: 2 (over x), rd: 2 (over core).
Axes of the slice: x: 2, y: 2, z: 4, core: 2. Of those that a mesh axis runs over, the one named last changes fastest.
Arguments:
- images: bfloat16 [2048, 4096], P(('groups', 'cls', 'img', 'rd')), parts along dimension 0, may hold values from -9 to 9
- counts: int32 [32, 4], P(('groups', 'cls', 'img', 'rd')), parts along dimension 0, may hold values from 1 to 31, as said below
- owners: int32 [32, 4], P(('groups', 'cls', 'img', 'rd')), parts along dimension 0, may hold values from 0 to 1, as said below
- references: bfloat16 [32, 4096], P(('groups', 'cls')), parts along dimension 0, may hold values from -1 to 1
Outputs:
- class_means: float32 [32, 4096], P(('groups', 'cls')), parts along dimension 0
- class_weights: float32 [32], P(('groups', 'cls')), parts along dimension 0
- loglik: float32 [2048], P(('groups', 'cls', 'img', 'rd')), parts along dimension 0
The draws below stay inside these ranges and needn't reach their ends.
There are 2 independent parts, one for each index of `groups`. The reference program is written for one: setup_inputs(seed, part) draws one part's arguments, and reference() takes and returns one part's arrays. A program takes and returns all parts, laid end to end along the dimension named above; each array names one. Nothing has to cross between parts.
Inputs may be any that keep to these rules, and one draw needn't show every extreme that they name: Each micrograph holds 1 or more particles; a reader's used rows number the sum of its counts, at most 64. At most 32 of a reader's particles have one owner; for every reader exactly 32 go to one owner, and that owner is the same for all readers with the same cls and rd index. `owners`: every owner is named by exactly two micrographs of each reader.
All inputs are finite; a program needn't handle non-finite values.
Results may differ from the reference program's by a relative error of at most 0.0024.
Values may be sent and summed in bfloat16 or wider, within the bound.
No kernel may reach another device: no remote copies, remote signals or barrier semaphores. Data moves between devices by JAX's collectives and lax.ppermute only.
A program may use at most 128 MiB of HBM per device.

```python
import jax
import jax.numpy as jnp
from jax import lax

BOX = 64
PIX = 4096
ROTS = 8
CLASSES = 16
CAP = 32
READ_DEV = 64
MIC_DEV = 4
READERS = 16
PARTICLES = 1024
N_CLS = 4
N_IMG = 2
N_RD = 2


def reference_base(key):
    return jnp.clip(jax.random.normal(key, (CLASSES, PIX), jnp.float32), -3.0, 3.0) * (2.0 / BOX)


def routing_draw(key):
    key_list = jax.random.split(jax.random.fold_in(key, 101), 4)
    owner_count = MIC_DEV // 2
    favored = jax.random.randint(key_list[0], (N_CLS, 1, N_RD), 0, owner_count)
    favored = jnp.broadcast_to(favored, (N_CLS, N_IMG, N_RD)).reshape(READERS)
    owner_ids = jnp.arange(owner_count, dtype=jnp.int32)
    is_favored = owner_ids[None, :] == favored[:, None]
    load_sizes = jax.random.randint(key_list[1], (READERS, owner_count), 2, CAP // 2 + 2)
    load_sizes = jnp.where(is_favored, CAP, load_sizes)
    first_part = jax.random.randint(key_list[2], (READERS, owner_count), 1, load_sizes)
    first_part = jnp.where(is_favored, 1, first_part)
    paired = jnp.stack([first_part, load_sizes - first_part], axis=2).reshape(READERS, MIC_DEV)
    row_keys = jax.random.split(key_list[3], READERS)
    shuffle = jax.vmap(lambda row_key: jax.random.permutation(row_key, MIC_DEV))(row_keys)
    counts_out = jnp.take_along_axis(paired, shuffle, axis=1).astype(jnp.int32)
    owners_out = (shuffle // 2).astype(jnp.int32)
    return (counts_out, owners_out)


def draw_counts(key, part):
    shared = routing_draw(key)
    return shared[0]


def draw_owners(key, part):
    shared = routing_draw(key)
    return shared[1]


def draw_references(key, part):
    class_base = reference_base(key)
    return class_base.astype(jnp.bfloat16)


def draw_images(key, part):
    key = jax.random.fold_in(key, 9)
    key_list = jax.random.split(key, 1)
    image_field = jnp.clip(jax.random.normal(key_list[0], (PARTICLES, PIX), jnp.float32), -4.0, 4.0)
    return image_field.astype(jnp.bfloat16)


def setup_inputs(seed: int = 0, part: int = 0) -> dict:
    key_of = jax.random.split(jax.random.key(seed), 5)
    part_splits = jax.random.split(jax.random.fold_in(key_of[4], part), 5)
    return {
        "images": draw_images(jax.random.fold_in(jax.random.fold_in(key_of[4], part), 71), part),
        "counts": draw_counts(jax.random.fold_in(jax.random.fold_in(key_of[4], part), 71), part),
        "owners": draw_owners(jax.random.fold_in(jax.random.fold_in(key_of[4], part), 71), part),
        "references": draw_references(jax.random.fold_in(jax.random.fold_in(key_of[4], part), 71), part),
    }


def turn_image(field, turn_index):
    square = field.reshape(field.shape[:-1] + (BOX, BOX))
    if turn_index >= 4:
        square = jnp.flip(square, -1)
    square = jnp.rot90(square, turn_index % 4, axes=(-2, -1))
    return square.reshape(field.shape)


def turn_back(field, turn_index):
    square = field.reshape(field.shape[:-1] + (BOX, BOX))
    square = jnp.rot90(square, -(turn_index % 4), axes=(-2, -1))
    if turn_index >= 4:
        square = jnp.flip(square, -1)
    return square.reshape(field.shape)


def slot_table(count_row, owner_row):
    mic_count = count_row.shape[0]
    ends = jnp.cumsum(count_row).astype(jnp.int32)
    position = jnp.arange(READ_DEV, dtype=jnp.int32)
    micrograph = jnp.sum((position[:, None] >= ends[None, :]).astype(jnp.int32), axis=1)
    usable = position < ends[mic_count - 1]
    matches = micrograph[:, None] == jnp.arange(mic_count, dtype=jnp.int32)[None, :]
    target = jnp.sum(jnp.where(matches, owner_row[None, :], 0), axis=1).astype(jnp.int32)
    earlier = (target[:, None] == target[None, :]) & usable[None, :] & (position[None, :] < position[:, None])
    ranking = jnp.sum(earlier.astype(jnp.int32), axis=1)
    slot_index = jnp.where(usable, target * CAP + ranking, -1)
    placing = slot_index[None, :] == jnp.arange(READ_DEV, dtype=jnp.int32)[:, None]
    return usable, placing


def reference(images, counts, owners, references):
    turned = jnp.stack([turn_image(references, turn_index) for turn_index in range(ROTS)], axis=1).reshape(CLASSES * ROTS, PIX)
    squares = jnp.repeat(jnp.sum(references.astype(jnp.float32) ** 2, axis=1), ROTS)
    blocks = images.reshape(READERS, READ_DEV, PIX)
    usable, placing = jax.vmap(slot_table)(counts, owners)

    def visit(carry, item):
        particle_rows, live_rows = item
        inner = lax.dot_general(particle_rows, turned, (((1,), (1,)), ((), ())), preferred_element_type=jnp.float32)
        scores = inner - 0.5 * squares[None, :]
        highest = jnp.max(scores, axis=1, keepdims=True)
        total = jnp.log(jnp.sum(jnp.exp(scores - highest), axis=1, keepdims=True)) + highest
        weights = jnp.where(live_rows[:, None], jnp.exp(scores - total), 0.0).astype(jnp.bfloat16)
        summed = carry[0] + lax.dot_general(weights, particle_rows, (((0,), (0,)), ((), ())), preferred_element_type=jnp.float32)
        column_sums = carry[1] + jnp.sum(weights.astype(jnp.float32), axis=0)
        row_loglik = jnp.where(live_rows, total[:, 0], 0.0)
        return (summed, column_sums), row_loglik

    start_sums = (jnp.zeros((CLASSES * ROTS, PIX), jnp.float32), jnp.zeros((CLASSES * ROTS,), jnp.float32))
    (summed, column_sums), row_loglik = lax.scan(visit, start_sums, (blocks, usable))
    summed = summed.reshape(CLASSES, ROTS, PIX)
    class_sums = turn_back(summed[:, 0], 0)
    for turn_index in range(1, ROTS):
        class_sums = class_sums + turn_back(summed[:, turn_index], turn_index)
    class_weights = jnp.sum(column_sums.reshape(CLASSES, ROTS), axis=1)
    class_means = class_sums / (class_weights[:, None] + 1.0)
    packed = jnp.sum(jnp.where(placing, row_loglik[:, None, :], 0.0), axis=-1)
    loglik = packed.reshape(N_CLS, N_IMG, N_RD, N_IMG, CAP).transpose(0, 3, 2, 1, 4).reshape(PARTICLES)
    return class_means, class_weights, loglik
```

```python
import functools

import jax
import jax.numpy as jnp
from jax import lax
from jax.experimental import pallas as pl
from jax.experimental.pallas import tpu as pltpu
from jax.sharding import PartitionSpec as P

BOX = 64
ROTS = 8
LANES = 128
PAIR = LANES // BOX
LINKED = ("cls", "img", "rd")
F32 = jnp.float32
BF16 = jnp.bfloat16


def rolled(tile, by):
    return jnp.concatenate([tile[:, by:], tile[:, :by]], axis=1)


def turn_kernel(own_ref, other_ref, out_ref, wide_ref):
    pixels = own_ref.shape[1]
    for block in range(pixels // LANES):
        span = slice(block * LANES, (block + 1) * LANES)
        tile = jnp.concatenate([own_ref[:, span], other_ref[:, span]], axis=0)
        tile = tile.astype(F32).T
        wide_ref[span, :] = tile
        out_ref[span, :LANES] = tile.astype(BF16)
    for column in range(BOX):
        out_ref[column * BOX:(column + 1) * BOX, LANES:] = wide_ref[
            pl.ds(column, BOX, stride=BOX), :
        ].astype(BF16)


def three_parts(value):
    high = value.astype(BF16).astype(F32)
    rest = value - high
    middle = rest.astype(BF16).astype(F32)
    return high, middle, (rest - middle).astype(BF16).astype(F32)


def slot_column(table_ref, rows, capacity):
    mic_count = table_ref.shape[1] // 2
    position = lax.broadcasted_iota(jnp.int32, (rows, 1), 0)
    slot = jnp.full((rows, 1), -1, jnp.int32)
    start = jnp.int32(0)
    for mic in range(mic_count):
        owner = table_ref[0, mic_count + mic]
        before = jnp.int32(0)
        for earlier in range(mic):
            same = table_ref[0, mic_count + earlier] == owner
            before = before + jnp.where(same, table_ref[0, earlier], 0)
        stop = start + table_ref[0, mic]
        inside = (position >= start) & (position < stop)
        slot = jnp.where(inside, position + (owner * capacity + before - start), slot)
        start = stop
    return slot, start


def weigh_kernel(capacity, core_ref, table_ref, other_table_ref, one_ref, two_ref, three_ref, own_ref,
                 images_ref, first_ref, second_ref, total_ref, flipped_ref, sums_ref):
    core = core_ref[0]
    per_dev, pixels = own_ref.shape
    classes = 4 * per_dev
    blocks = pixels // LANES
    rows = LANES // 2
    half = classes // 2
    block_of = [slice(b * LANES, (b + 1) * LANES) for b in range(blocks)]
    row_of = lax.broadcasted_iota(jnp.int32, (LANES, LANES), 0)
    column_of = lax.broadcasted_iota(jnp.int32, (LANES, LANES), 1)
    within = (row_of // BOX) * BOX + (BOX - 1 - row_of % BOX)
    mirror = (column_of == within).astype(BF16)

    refs = jnp.concatenate([one_ref[...].astype(F32), two_ref[...].astype(F32),
                            three_ref[...].astype(F32), own_ref[...].astype(F32)], axis=0)
    squares = jnp.sum(refs * refs, axis=1, keepdims=True)
    stacked = jnp.concatenate([refs[:, b] for b in block_of], axis=0)
    mirrored = jnp.dot(stacked.astype(BF16), mirror, preferred_element_type=F32)
    for b in range(blocks):
        part = slice(b * classes, (b + 1) * classes)
        plain, turned = stacked[part], mirrored[part]
        back = block_of[blocks - 1 - b]
        flipped_ref[0:classes, block_of[b]] = plain.astype(BF16)
        flipped_ref[classes:2 * classes, block_of[b]] = turned.astype(BF16)
        flipped_ref[2 * classes:3 * classes, back] = rolled(plain, BOX).astype(BF16)
        flipped_ref[3 * classes:4 * classes, back] = rolled(turned, BOX).astype(BF16)

    inner = jnp.dot(flipped_ref[...], images_ref[...], preferred_element_type=F32)
    scores = inner - 0.5 * jnp.concatenate([squares] * 4, axis=0)
    highest = jnp.max(scores, axis=0, keepdims=True)
    highest = jnp.maximum(highest[:, :LANES], highest[:, LANES:])
    shifted = jnp.exp(scores - jnp.concatenate([highest, highest], axis=1))
    summed = jnp.sum(shifted, axis=0, keepdims=True)
    total = jnp.log(summed[:, :LANES] + summed[:, LANES:]) + highest

    slot, used = slot_column(table_ref, rows, capacity)
    other_slot, other_used = slot_column(other_table_ref, rows, capacity)
    lane = lax.broadcasted_iota(jnp.int32, (1, LANES), 1)
    live = (lane < used) | ((lane >= rows) & (lane < rows + other_used))
    live = jnp.concatenate([live, live], axis=1)
    weights = jnp.where(live, jnp.exp(scores - jnp.concatenate([total, total], axis=1)), 0.0)
    weights = weights.astype(BF16).astype(F32)
    chosen = jnp.concatenate(
        [
            jnp.where(core == 0, weights[f * classes:f * classes + half],
                      weights[f * classes + half:(f + 1) * classes])
            for f in range(4)
        ],
        axis=0,
    )
    sums_ref[...] = lax.dot_general(
        chosen.astype(BF16), images_ref[...], (((1,), (1,)), ((), ())), preferred_element_type=F32
    )
    straight, swapped = [], []
    for b in range(blocks):
        back = block_of[blocks - 1 - b]
        straight.append(sums_ref[0:half, block_of[b]] + rolled(sums_ref[2 * half:3 * half, back], BOX))
        swapped.append(sums_ref[half:2 * half, block_of[b]] + rolled(sums_ref[3 * half:, back], BOX))
    swapped = jnp.concatenate(swapped, axis=0)
    upper = swapped.astype(BF16)
    lower = (swapped - upper.astype(F32)).astype(BF16)
    swapped = jnp.dot(upper, mirror, preferred_element_type=F32) + jnp.dot(
        lower, mirror, preferred_element_type=F32
    )
    for b in range(blocks):
        both = straight[b] + swapped[b * half:(b + 1) * half]
        first_ref[:, block_of[b]] = both[:per_dev].astype(BF16)
        second_ref[:, block_of[b]] = both[per_dev:].astype(BF16)

    per_class = jnp.sum(chosen, axis=1, keepdims=True)
    per_class = per_class[0:half] + per_class[half:2 * half] + per_class[2 * half:3 * half] + per_class[3 * half:]
    high, middle, low = three_parts(per_class)
    lanes = lax.broadcasted_iota(jnp.int32, (half, LANES), 1)
    sent = jnp.where(lanes == 0, high, jnp.where(lanes == 1, middle, jnp.where(lanes == 2, low, 0.0)))
    extra = slice(pixels, pixels + LANES)
    first_ref[:, extra] = sent[:per_dev].astype(BF16)
    second_ref[:, extra] = sent[per_dev:].astype(BF16)

    column = jnp.concatenate([slot, jnp.where(other_slot < 0, -1, other_slot + rows)], axis=0)
    placing = (column == column_of).astype(BF16)
    high, middle, low = three_parts(total)
    pieces = jnp.concatenate([high, middle, low, jnp.zeros((5, LANES), F32)], axis=0)
    pieces = jnp.dot(pieces.astype(BF16), placing, preferred_element_type=F32)
    total_ref[...] = pieces[0:1] + pieces[1:2] + pieces[2:3]
    last = slice(pixels + LANES, pixels + 2 * LANES)
    first_ref[:, last] = jnp.zeros((per_dev, LANES), BF16)
    second_ref[:, last] = pieces[:per_dev].astype(BF16)


def add_kernel(core_ref, one_ref, two_ref, three_ref, four_ref, own_ref, out_ref):
    pixels = out_ref.shape[1] - LANES
    middle = jnp.where(core_ref[0] == 0, three_ref[:, :pixels].astype(F32), own_ref[:, :pixels].astype(F32))
    out_ref[:, :pixels] = (one_ref[:, :pixels].astype(F32) + two_ref[:, :pixels].astype(F32)) + (
        middle + four_ref[:, :pixels].astype(F32)
    )
    pieces = four_ref[:, pixels:].astype(F32)
    out_ref[:, pixels:] = jnp.broadcast_to(pieces[0:1] + pieces[1:2] + pieces[2:3], (out_ref.shape[0], LANES))


def finish_kernel(place_ref, own_ref, other_ref, total_ref, means_ref, weights_ref, loglik_ref):
    core, image = place_ref[0], place_ref[1]
    per_dev, pixels = means_ref.shape
    capacity = loglik_ref.shape[1] // 2
    extra = slice(pixels, pixels + LANES)
    count = own_ref[:, extra] + other_ref[:, extra]
    count = count[:, 0:1] + count[:, 1:2] + count[:, 2:3]
    means_ref[...] = (own_ref[:, :pixels] + other_ref[:, :pixels]) / (count + 1.0)
    across = lax.broadcasted_iota(jnp.int32, (per_dev, per_dev), 1)
    down = lax.broadcasted_iota(jnp.int32, (per_dev, per_dev), 0)
    weights_ref[...] = jnp.sum(jnp.where(across == down, count, 0.0), axis=0, keepdims=True)
    last = slice(pixels + LANES, pixels + 2 * LANES)
    arrived = jnp.where(core == 0, rolled(other_ref[0:1, last], 2 * capacity), own_ref[0:1, last])
    mine = total_ref[...]
    arrived = jnp.where(image == 0, arrived[:, :capacity], arrived[:, capacity:2 * capacity])
    mine = jnp.where(image == 0, mine[:, :capacity], mine[:, capacity:2 * capacity])
    loglik_ref[:, :capacity] = jnp.where(image == 0, mine, arrived)
    loglik_ref[:, capacity:] = jnp.where(image == 0, arrived, mine)


def passed_along(array, axis, by):
    devices = lax.axis_size(axis)
    return lax.ppermute(array, axis, [(i, (i + by) % devices) for i in range(devices)])


def turn_image(field, turn_index):
    square = field.reshape(field.shape[:-1] + (BOX, BOX))
    if turn_index >= 4:
        square = jnp.flip(square, -1)
    square = jnp.rot90(square, turn_index % 4, axes=(-2, -1))
    return square.reshape(field.shape)


def turn_back(field, turn_index):
    square = field.reshape(field.shape[:-1] + (BOX, BOX))
    square = jnp.rot90(square, -(turn_index % 4), axes=(-2, -1))
    if turn_index >= 4:
        square = jnp.flip(square, -1)
    return square.reshape(field.shape)


def slot_table(count_row, owner_row, read_rows, capacity):
    mic_count = count_row.shape[0]
    ends = jnp.cumsum(count_row)
    position = jnp.arange(read_rows, dtype=jnp.int32)
    micrograph = jnp.sum((position[:, None] >= ends[None, :]).astype(jnp.int32), axis=1)
    usable = position < ends[mic_count - 1]
    matches = micrograph[:, None] == jnp.arange(mic_count, dtype=jnp.int32)[None, :]
    target = jnp.sum(jnp.where(matches, owner_row[None, :], 0), axis=1)
    earlier = (
        (target[:, None] == target[None, :])
        & usable[None, :]
        & (position[None, :] < position[:, None])
    )
    ranking = jnp.sum(earlier.astype(jnp.int32), axis=1)
    slot_index = jnp.where(usable, target * capacity + ranking, -1)
    placing = slot_index[None, :] == jnp.arange(read_rows, dtype=jnp.int32)[:, None]
    return (usable, placing)


def class_scores(particle_rows, piece):
    pixels = piece.shape[1]
    turned = jnp.stack(
        [turn_image(piece, turn_index) for turn_index in range(ROTS)], axis=1
    ).reshape(-1, pixels)
    squares = jnp.sum(piece.astype(jnp.float32) ** 2, axis=1)
    inner = lax.dot_general(
        particle_rows, turned, (((1,), (1,)), ((), ())), preferred_element_type=jnp.float32
    )
    return inner - 0.5 * jnp.repeat(squares, ROTS)[None, :]


def class_block(weights, particle_rows, first_class, class_count):
    chosen = lax.dynamic_slice_in_dim(weights, first_class * ROTS, class_count * ROTS, 1)
    summed = lax.dot_general(
        chosen, particle_rows, (((0,), (0,)), ((), ())), preferred_element_type=jnp.float32
    )
    summed = summed.reshape(class_count, ROTS, summed.shape[1])
    result = turn_back(summed[:, 0], 0)
    for turn_index in range(1, ROTS):
        result = result + turn_back(summed[:, turn_index], turn_index)
    return result


def local(images, counts, owners, references):
    read_rows, pixels = images.shape
    n_img = lax.axis_size("img")
    n_cls = lax.axis_size("cls")
    capacity = read_rows // n_img
    per_dev = references.shape[0]
    classes = per_dev * n_cls
    usable, placing = slot_table(counts[0], owners[0], read_rows, capacity)
    packed = jnp.dot(
        placing.astype(jnp.bfloat16), images, preferred_element_type=jnp.float32
    ).astype(jnp.bfloat16)
    filled = jnp.sum(placing.astype(jnp.float32), axis=1).astype(jnp.bfloat16)
    moved, arrived = (
        lax.all_to_all(
            packed.reshape(n_img, capacity, pixels), "img", split_axis=0, concat_axis=0, tiled=True
        ),
        lax.all_to_all(
            filled.reshape(n_img, capacity), "img", split_axis=0, concat_axis=0, tiled=True
        ),
    )
    particle_rows = moved.reshape(read_rows, pixels)
    live_rows = arrived.reshape(read_rows) > 0
    scores = class_scores(particle_rows, lax.all_gather(references, "cls", axis=0, tiled=True))
    highest = jnp.max(scores, axis=1, keepdims=True)
    total = jnp.log(jnp.sum(jnp.exp(scores - highest), axis=1, keepdims=True)) + highest
    weights = jnp.where(live_rows[:, None], jnp.exp(scores - total), 0.0).astype(jnp.bfloat16)
    row_loglik = jnp.where(live_rows, total[:, 0], 0.0)
    column_sums = jnp.sum(
        jnp.sum(weights.astype(jnp.float32), axis=0).reshape(classes, ROTS), axis=1
    )
    totals = lax.psum(column_sums, ("cls", "img", "rd"))
    device_index = lax.axis_index("cls")
    own_totals = lax.dynamic_slice_in_dim(totals, device_index * per_dev, per_dev)

    def cycle_stop(stop_index, carried):
        block = (device_index - 1 - stop_index) % n_cls
        carried = carried + class_block(weights, particle_rows, block * per_dev, per_dev)
        return passed_along(carried, "cls", 1)

    carried = lax.fori_loop(0, n_cls - 1, cycle_stop, jnp.zeros((per_dev, pixels), jnp.float32))
    class_sums = carried + class_block(weights, particle_rows, device_index * per_dev, per_dev)
    class_sums = lax.psum(class_sums, ("img", "rd"))
    class_means = class_sums / (own_totals[:, None] + 1.0)
    return (class_means, own_totals, row_loglik)


def swapped_by(array, by, axes=LINKED):
    devices = 1
    for axis in axes:
        devices = devices * lax.axis_size(axis)
    pairs = []
    for i in range(devices):
        step = by(i & 1) if callable(by) else by
        if step:
            pairs.append((i, i ^ step))
    return lax.ppermute(array, axes, pairs)


def call(kernel, outs, args, scalars, scratch=()):
    specs = [pl.BlockSpec(memory_space=pltpu.SMEM)] * scalars
    specs += [pl.BlockSpec(memory_space=pltpu.VMEM)] * (len(args) - scalars)
    return pl.pallas_call(
        kernel,
        out_shape=outs,
        in_specs=specs,
        out_specs=jax.tree.map(lambda _: pl.BlockSpec(memory_space=pltpu.VMEM), outs),
        scratch_shapes=list(scratch),
        compiler_params=pltpu.CompilerParams(vmem_limit_bytes=32 * 1024 * 1024),
    )(*args)


def direct(images, counts, owners, references):
    read_rows, pixels = images.shape
    capacity = read_rows // lax.axis_size("img")
    per_dev = references.shape[0]
    core = lax.axis_index("rd")
    place = jnp.stack([core, lax.axis_index("img")]).astype(jnp.int32)
    table = jnp.concatenate([counts, owners], axis=1)
    other_images = swapped_by(images, 1, ("rd",))
    other_table = swapped_by(table, 1, ("rd",))
    near, far, cross = [swapped_by(references, k, ("cls",)) for k in (1, 2, 3)]
    shape = jax.ShapeDtypeStruct
    turned = call(turn_kernel, shape((pixels, 2 * LANES), BF16), (images, other_images), 0,
                  [pltpu.VMEM((pixels, LANES), F32)])
    wide = pixels + 2 * LANES
    first, second, totals = call(
        functools.partial(weigh_kernel, capacity),
        (shape((per_dev, wide), BF16), shape((per_dev, wide), BF16), shape((1, LANES), F32)),
        (place, table, other_table, near, far, cross, references, turned), 3,
        [pltpu.VMEM((16 * per_dev, pixels), BF16), pltpu.VMEM((8 * per_dev, pixels), F32)],
    )
    one = swapped_by(first, lambda rd: 12 if rd else 4)
    two = swapped_by(first, lambda rd: 14 if rd else 6)
    three = swapped_by(second, lambda rd: 0 if rd else 8)
    four = swapped_by(second, lambda rd: 2 if rd else 10)
    summed = call(add_kernel, shape((per_dev, wide), F32), (place, one, two, three, four, second), 1)
    other = swapped_by(summed, 1, ("rd",))
    means, weights, loglik = call(
        finish_kernel,
        (shape((per_dev, pixels), F32), shape((1, per_dev), F32), shape((1, read_rows), F32)),
        (place, summed, other, totals), 1,
    )
    return means, weights.reshape(per_dev), loglik.reshape(read_rows)


def solution(mesh):
    sizes = mesh.shape
    small = sizes["cls"] == 4 and sizes["img"] == 2 and sizes["rd"] == 2
    placed = (
        P(("groups", "cls", "img", "rd"), None),
        P(("groups", "cls", "img", "rd"), None),
        P(("groups", "cls", "img", "rd"), None),
        P(("groups", "cls"), None),
    )
    return jax.shard_map(
        direct if small else local,
        mesh=mesh,
        in_specs=placed,
        out_specs=(
            P(("groups", "cls"), None),
            P(("groups", "cls")),
            P(("groups", "cls", "img", "rd")),
        ),
        check_vma=False,
    )
```

```python
import functools

import jax
import jax.numpy as jnp
from jax import lax
from jax.experimental import pallas as pl
from jax.experimental.pallas import tpu as pltpu
from jax.sharding import PartitionSpec as P

BOX = 64
ROTS = 8
LANES = 128
PAIR = LANES // BOX
LINKED = ("cls", "img", "rd")
F32 = jnp.float32
BF16 = jnp.bfloat16


def rolled(tile, by):
    return jnp.concatenate([tile[:, by:], tile[:, :by]], axis=1)


def turn_kernel(own_hbm, other_ref, out_ref, own_ref, wide_ref, arrived):
    pixels = other_ref.shape[1]
    pieces = arrived.shape[0]
    width = pixels // pieces
    copies = []
    for piece in range(pieces):
        span = pl.ds(piece * width, width)
        copies.append(pltpu.make_async_copy(own_hbm.at[:, span], own_ref.at[:, span], arrived.at[piece]))
        copies[-1].start()
    for block in range(pixels // LANES):
        if block * LANES % width == 0:
            copies[block * LANES // width].wait()
        span = slice(block * LANES, (block + 1) * LANES)
        tile = jnp.concatenate([own_ref[:, span], other_ref[:, span]], axis=0)
        tile = tile.astype(F32).T
        wide_ref[span, :] = tile
        out_ref[span, :LANES] = tile.astype(BF16)
    for column in range(BOX):
        out_ref[column * BOX:(column + 1) * BOX, LANES:] = wide_ref[
            pl.ds(column, BOX, stride=BOX), :
        ].astype(BF16)


def three_parts(value):
    high = value.astype(BF16).astype(F32)
    rest = value - high
    middle = rest.astype(BF16).astype(F32)
    return high, middle, (rest - middle).astype(BF16).astype(F32)


def slot_row(counts_ref, owners_ref, capacity):
    mic_count = counts_ref.shape[1]
    position = lax.broadcasted_iota(jnp.int32, (1, LANES), 1)
    slot = jnp.full((1, LANES), -1, jnp.int32)
    start = jnp.int32(0)
    for mic in range(mic_count):
        owner = owners_ref[0, mic]
        before = jnp.int32(0)
        for earlier in range(mic):
            before = before + jnp.where(owners_ref[0, earlier] == owner, counts_ref[0, earlier], 0)
        stop = start + counts_ref[0, mic]
        inside = (position >= start) & (position < stop)
        slot = jnp.where(inside, position + (owner * capacity + before - start), slot)
        start = stop
    return slot


def mirror_of_rows():
    row = lax.broadcasted_iota(jnp.int32, (LANES, LANES), 0)
    column = lax.broadcasted_iota(jnp.int32, (LANES, LANES), 1)
    return (column == (row // BOX) * BOX + (BOX - 1 - row % BOX)).astype(BF16)


def spans(pixels):
    return [slice(b * LANES, (b + 1) * LANES) for b in range(pixels // LANES)]


def score_kernel(capacity, counts_ref, owners_ref, first_ref, second_ref, own_ref, images_ref, scores_ref, stats_ref, flipped_ref):
    per_dev, pixels = own_ref.shape
    half = 2 * per_dev
    block_of = spans(pixels)
    second = jnp.where(lax.axis_index("rd") == 0, second_ref[...].astype(F32), own_ref[...].astype(F32))
    refs = jnp.concatenate([first_ref[...].astype(F32), second], axis=0)
    squares = jnp.sum(refs * refs, axis=1, keepdims=True)
    stacked = jnp.concatenate([refs[:, b] for b in block_of], axis=0)
    mirrored = jnp.dot(stacked.astype(BF16), mirror_of_rows(), preferred_element_type=F32)
    for b in range(len(block_of)):
        part = slice(b * half, (b + 1) * half)
        both = jnp.concatenate([stacked[part], mirrored[part]], axis=0)
        flipped_ref[:2 * half, block_of[b]] = both.astype(BF16)
        flipped_ref[2 * half:, block_of[-1 - b]] = rolled(both, BOX).astype(BF16)
    inner = jnp.dot(flipped_ref[...], images_ref[...], preferred_element_type=F32)
    scores = inner - 0.5 * jnp.concatenate([squares] * 4, axis=0)
    scores_ref[...] = scores
    highest = jnp.max(scores, axis=0, keepdims=True)
    highest = jnp.maximum(highest[:, :LANES], highest[:, LANES:])
    summed = jnp.sum(jnp.exp(scores - jnp.concatenate([highest, highest], axis=1)), axis=0, keepdims=True)
    summed = summed[:, :LANES] + summed[:, LANES:]
    slot = slot_row(counts_ref, owners_ref, capacity).astype(F32)
    stats_ref[...] = jnp.concatenate([highest, summed, slot, jnp.zeros((5, LANES), F32)], axis=0)


def weigh_kernel(scores_ref, stats_ref, other_stats_ref, images_ref, first_ref, second_ref, total_ref, sums_ref):
    per_dev = first_ref.shape[0]
    pixels = images_ref.shape[0]
    rows = LANES // 2
    half = 2 * per_dev
    block_of = spans(pixels)
    scores = scores_ref[...]
    other = rolled(other_stats_ref[...], BOX)
    highest = jnp.maximum(stats_ref[0:1], other[0:1])
    summed = stats_ref[1:2] * jnp.exp(stats_ref[0:1] - highest) + other[1:2] * jnp.exp(other[0:1] - highest)
    total = jnp.log(summed) + highest

    lane = lax.broadcasted_iota(jnp.int32, (1, LANES), 1)
    slot = jnp.where(lane < rows, stats_ref[2:3], other[2:3]).astype(jnp.int32)
    live = slot >= 0
    slot = jnp.where(live & (lane >= rows), slot + rows, slot)
    live = jnp.concatenate([live, live], axis=1)
    weights = jnp.where(live, jnp.exp(scores - jnp.concatenate([total, total], axis=1)), 0.0).astype(BF16)
    sums_ref[...] = lax.dot_general(
        weights, images_ref[...], (((1,), (1,)), ((), ())), preferred_element_type=F32
    )
    straight, swapped = [], []
    for b in range(len(block_of)):
        back = block_of[-1 - b]
        straight.append(sums_ref[0:half, block_of[b]] + rolled(sums_ref[2 * half:3 * half, back], BOX))
        swapped.append(sums_ref[half:2 * half, block_of[b]] + rolled(sums_ref[3 * half:, back], BOX))
    swapped = jnp.concatenate(swapped, axis=0)
    upper = swapped.astype(BF16)
    lower = (swapped - upper.astype(F32)).astype(BF16)
    mirror = mirror_of_rows()
    swapped = jnp.dot(upper, mirror, preferred_element_type=F32) + jnp.dot(
        lower, mirror, preferred_element_type=F32
    )
    for b in range(len(block_of)):
        both = straight[b] + swapped[b * half:(b + 1) * half]
        first_ref[:, block_of[b]] = both[:per_dev].astype(BF16)
        second_ref[:, block_of[b]] = both[per_dev:].astype(BF16)

    per_class = jnp.sum(weights.astype(F32), axis=1, keepdims=True)
    per_class = per_class[0:half] + per_class[half:2 * half] + per_class[2 * half:3 * half] + per_class[3 * half:]
    high, middle, low = three_parts(per_class)
    lanes = lax.broadcasted_iota(jnp.int32, (half, LANES), 1)
    sent = jnp.where(lanes == 0, high, jnp.where(lanes == 1, middle, jnp.where(lanes == 2, low, 0.0)))
    extra = slice(pixels, pixels + LANES)
    first_ref[:, extra] = sent[:per_dev].astype(BF16)
    second_ref[:, extra] = sent[per_dev:].astype(BF16)

    placing = (slot == lax.broadcasted_iota(jnp.int32, (LANES, LANES), 0)).astype(BF16)
    pieces = jnp.concatenate([*three_parts(total), jnp.zeros((5, LANES), F32)], axis=0)
    pieces = lax.dot_general(
        pieces.astype(BF16), placing, (((1,), (1,)), ((), ())), preferred_element_type=F32
    )
    total_ref[...] = pieces[0:1] + pieces[1:2] + pieces[2:3]
    last = slice(pixels + LANES, pixels + 2 * LANES)
    first_ref[:, last] = jnp.zeros((per_dev, LANES), BF16)
    second_ref[:, last] = pieces[:per_dev].astype(BF16)


def add_kernel(two_ref, one_ref, three_ref, four_ref, own_ref, out_ref):
    pixels = out_ref.shape[1] - LANES
    middle = jnp.where(lax.axis_index("rd") == 0, three_ref[:, :pixels].astype(F32), own_ref[:, :pixels].astype(F32))
    out_ref[:, :pixels] = (one_ref[:, :pixels].astype(F32) + two_ref[:, :pixels].astype(F32)) + (
        middle + four_ref[:, :pixels].astype(F32)
    )
    pieces = four_ref[:, pixels:].astype(F32)
    out_ref[:, pixels:] = jnp.broadcast_to(pieces[0:1] + pieces[1:2] + pieces[2:3], (out_ref.shape[0], LANES))


def finish_kernel(own_ref, other_ref, total_ref, means_hbm, weights_hbm, loglik_hbm,
                  means_ref, weights_ref, loglik_ref, sent):
    per_dev, pixels = means_ref.shape
    capacity = loglik_ref.shape[1] // 2
    extra = slice(pixels, pixels + LANES)
    last = slice(pixels + LANES, pixels + 2 * LANES)
    pieces = sent.shape[0] - 2
    width = pixels // pieces
    count = own_ref[:, extra] + other_ref[:, extra]
    count = count[:, 0:1] + count[:, 1:2] + count[:, 2:3]
    scale = 1.0 / (count + 1.0)
    copies = []
    for piece in range(pieces):
        span = pl.ds(piece * width, width)
        means_ref[:, span] = (own_ref[:, span] + other_ref[:, span]) * scale
        copies.append(pltpu.make_async_copy(means_ref.at[:, span], means_hbm.at[:, span], sent.at[piece]))
        copies[-1].start()
    across = lax.broadcasted_iota(jnp.int32, (per_dev, per_dev), 1)
    down = lax.broadcasted_iota(jnp.int32, (per_dev, per_dev), 0)
    weights_ref[...] = jnp.sum(jnp.where(across == down, count, 0.0), axis=0, keepdims=True)
    copies.append(pltpu.make_async_copy(weights_ref, weights_hbm, sent.at[pieces]))
    copies[-1].start()
    first = lax.axis_index("img") == 0
    arrived = jnp.where(
        lax.axis_index("rd") == 0, rolled(other_ref[0:1, last], 2 * capacity), own_ref[0:1, last]
    )
    arrived = jnp.where(first, arrived[:, :capacity], arrived[:, capacity:2 * capacity])
    mine = jnp.where(first, total_ref[:, :capacity], total_ref[:, capacity:2 * capacity])
    loglik_ref[:, :capacity] = jnp.where(first, mine, arrived)
    loglik_ref[:, capacity:] = jnp.where(first, arrived, mine)
    copies.append(pltpu.make_async_copy(loglik_ref, loglik_hbm, sent.at[pieces + 1]))
    copies[-1].start()
    for copy in copies:
        copy.wait()


def passed_along(array, axis, by):
    devices = lax.axis_size(axis)
    return lax.ppermute(array, axis, [(i, (i + by) % devices) for i in range(devices)])


def turn_image(field, turn_index):
    square = field.reshape(field.shape[:-1] + (BOX, BOX))
    if turn_index >= 4:
        square = jnp.flip(square, -1)
    square = jnp.rot90(square, turn_index % 4, axes=(-2, -1))
    return square.reshape(field.shape)


def turn_back(field, turn_index):
    square = field.reshape(field.shape[:-1] + (BOX, BOX))
    square = jnp.rot90(square, -(turn_index % 4), axes=(-2, -1))
    if turn_index >= 4:
        square = jnp.flip(square, -1)
    return square.reshape(field.shape)


def slot_table(count_row, owner_row, read_rows, capacity):
    mic_count = count_row.shape[0]
    ends = jnp.cumsum(count_row)
    position = jnp.arange(read_rows, dtype=jnp.int32)
    micrograph = jnp.sum((position[:, None] >= ends[None, :]).astype(jnp.int32), axis=1)
    usable = position < ends[mic_count - 1]
    matches = micrograph[:, None] == jnp.arange(mic_count, dtype=jnp.int32)[None, :]
    target = jnp.sum(jnp.where(matches, owner_row[None, :], 0), axis=1)
    earlier = (
        (target[:, None] == target[None, :])
        & usable[None, :]
        & (position[None, :] < position[:, None])
    )
    ranking = jnp.sum(earlier.astype(jnp.int32), axis=1)
    slot_index = jnp.where(usable, target * capacity + ranking, -1)
    placing = slot_index[None, :] == jnp.arange(read_rows, dtype=jnp.int32)[:, None]
    return (usable, placing)


def class_scores(particle_rows, piece):
    pixels = piece.shape[1]
    turned = jnp.stack(
        [turn_image(piece, turn_index) for turn_index in range(ROTS)], axis=1
    ).reshape(-1, pixels)
    squares = jnp.sum(piece.astype(jnp.float32) ** 2, axis=1)
    inner = lax.dot_general(
        particle_rows, turned, (((1,), (1,)), ((), ())), preferred_element_type=jnp.float32
    )
    return inner - 0.5 * jnp.repeat(squares, ROTS)[None, :]


def class_block(weights, particle_rows, first_class, class_count):
    chosen = lax.dynamic_slice_in_dim(weights, first_class * ROTS, class_count * ROTS, 1)
    summed = lax.dot_general(
        chosen, particle_rows, (((0,), (0,)), ((), ())), preferred_element_type=jnp.float32
    )
    summed = summed.reshape(class_count, ROTS, summed.shape[1])
    result = turn_back(summed[:, 0], 0)
    for turn_index in range(1, ROTS):
        result = result + turn_back(summed[:, turn_index], turn_index)
    return result


def local(images, counts, owners, references):
    read_rows, pixels = images.shape
    n_img = lax.axis_size("img")
    n_cls = lax.axis_size("cls")
    capacity = read_rows // n_img
    per_dev = references.shape[0]
    classes = per_dev * n_cls
    usable, placing = slot_table(counts[0], owners[0], read_rows, capacity)
    packed = jnp.dot(
        placing.astype(jnp.bfloat16), images, preferred_element_type=jnp.float32
    ).astype(jnp.bfloat16)
    filled = jnp.sum(placing.astype(jnp.float32), axis=1).astype(jnp.bfloat16)
    moved, arrived = (
        lax.all_to_all(
            packed.reshape(n_img, capacity, pixels), "img", split_axis=0, concat_axis=0, tiled=True
        ),
        lax.all_to_all(
            filled.reshape(n_img, capacity), "img", split_axis=0, concat_axis=0, tiled=True
        ),
    )
    particle_rows = moved.reshape(read_rows, pixels)
    live_rows = arrived.reshape(read_rows) > 0
    scores = class_scores(particle_rows, lax.all_gather(references, "cls", axis=0, tiled=True))
    highest = jnp.max(scores, axis=1, keepdims=True)
    total = jnp.log(jnp.sum(jnp.exp(scores - highest), axis=1, keepdims=True)) + highest
    weights = jnp.where(live_rows[:, None], jnp.exp(scores - total), 0.0).astype(jnp.bfloat16)
    row_loglik = jnp.where(live_rows, total[:, 0], 0.0)
    column_sums = jnp.sum(
        jnp.sum(weights.astype(jnp.float32), axis=0).reshape(classes, ROTS), axis=1
    )
    totals = lax.psum(column_sums, ("cls", "img", "rd"))
    device_index = lax.axis_index("cls")
    own_totals = lax.dynamic_slice_in_dim(totals, device_index * per_dev, per_dev)

    def cycle_stop(stop_index, carried):
        block = (device_index - 1 - stop_index) % n_cls
        carried = carried + class_block(weights, particle_rows, block * per_dev, per_dev)
        return passed_along(carried, "cls", 1)

    carried = lax.fori_loop(0, n_cls - 1, cycle_stop, jnp.zeros((per_dev, pixels), jnp.float32))
    class_sums = carried + class_block(weights, particle_rows, device_index * per_dev, per_dev)
    class_sums = lax.psum(class_sums, ("img", "rd"))
    class_means = class_sums / (own_totals[:, None] + 1.0)
    return (class_means, own_totals, row_loglik)


def swapped_by(array, by, axes=LINKED):
    devices = 1
    for axis in axes:
        devices = devices * lax.axis_size(axis)
    pairs = []
    for i in range(devices):
        step = by(i & 1) if callable(by) else by
        if step:
            pairs.append((i, i ^ step))
    return lax.ppermute(array, axes, pairs)


def call(kernel, outs, args, scalars=(), scratch=(), in_hbm=(), outs_in_hbm=False):
    specs = [
        pl.BlockSpec(memory_space=pltpu.SMEM if i in scalars else pltpu.HBM if i in in_hbm else pltpu.VMEM)
        for i in range(len(args))
    ]
    out_space = pltpu.HBM if outs_in_hbm else pltpu.VMEM
    return pl.pallas_call(
        kernel,
        out_shape=outs,
        in_specs=specs,
        out_specs=jax.tree.map(lambda _: pl.BlockSpec(memory_space=out_space), outs),
        scratch_shapes=list(scratch),
        compiler_params=pltpu.CompilerParams(vmem_limit_bytes=32 * 1024 * 1024),
    )(*args)


def direct(images, counts, owners, references):
    read_rows, pixels = images.shape
    capacity = read_rows // lax.axis_size("img")
    per_dev = references.shape[0]
    other_images = swapped_by(images, 1, ("rd",))
    ref_far = swapped_by(references, lambda rd: 12 if rd else 8)
    ref_near = swapped_by(references, 4)
    shape = jax.ShapeDtypeStruct
    turned = call(
        turn_kernel, shape((pixels, 2 * LANES), BF16), (images, other_images), (),
        [pltpu.VMEM((read_rows, pixels), BF16), pltpu.VMEM((pixels, LANES), F32), pltpu.SemaphoreType.DMA((4,))],
        in_hbm=(0,),
    )
    scores, stats = call(
        functools.partial(score_kernel, capacity),
        (shape((8 * per_dev, 2 * LANES), F32), shape((8, LANES), F32)),
        (counts, owners, ref_far, ref_near, references, turned), (0, 1),
        [pltpu.VMEM((8 * per_dev, pixels), BF16)],
    )
    other_stats = swapped_by(stats, 1, ("rd",))
    wide = pixels + 2 * LANES
    far, near, totals = call(
        weigh_kernel,
        (shape((per_dev, wide), BF16), shape((per_dev, wide), BF16), shape((1, LANES), F32)),
        (scores, stats, other_stats, turned), (), [pltpu.VMEM((8 * per_dev, pixels), F32)],
    )
    two = swapped_by(far, lambda rd: 14 if rd else 10)
    one = swapped_by(far, lambda rd: 12 if rd else 8)
    four = swapped_by(near, lambda rd: 2 if rd else 6)
    three = swapped_by(near, 4)
    summed = call(add_kernel, shape((per_dev, wide), F32), (two, one, three, four, near))
    other = swapped_by(summed, 1, ("rd",))
    outs = (shape((per_dev, pixels), F32), shape((1, per_dev), F32), shape((1, read_rows), F32))
    means, weights, loglik = call(
        finish_kernel, outs, (summed, other, totals), (),
        [pltpu.VMEM(out.shape, out.dtype) for out in outs] + [pltpu.SemaphoreType.DMA((6,))],
        outs_in_hbm=True,
    )
    return means, weights.reshape(per_dev), loglik.reshape(read_rows)


def solution(mesh):
    sizes = mesh.shape
    small = sizes["cls"] == 4 and sizes["img"] == 2 and sizes["rd"] == 2
    placed = (
        P(("groups", "cls", "img", "rd"), None),
        P(("groups", "cls", "img", "rd"), None),
        P(("groups", "cls", "img", "rd"), None),
        P(("groups", "cls"), None),
    )
    return jax.shard_map(
        direct if small else local,
        mesh=mesh,
        in_specs=placed,
        out_specs=(
            P(("groups", "cls"), None),
            P(("groups", "cls")),
            P(("groups", "cls", "img", "rd")),
        ),
        check_vma=False,
    )
```

```python
import functools

import jax
import jax.numpy as jnp
from jax import lax
from jax.experimental import pallas as pl
from jax.experimental.pallas import tpu as pltpu
from jax.sharding import PartitionSpec as P

BOX = 64
ROTS = 8
LANES = 128
PAIR = LANES // BOX
LINKED = ("cls", "img", "rd")
F32 = jnp.float32
BF16 = jnp.bfloat16


def rolled(tile, by):
    return jnp.concatenate([tile[:, by:], tile[:, :by]], axis=1)


def turn_kernel(own_hbm, other_ref, out_ref, own_ref, wide_ref, arrived):
    pixels = other_ref.shape[1]
    pieces = arrived.shape[0]
    width = pixels // pieces
    copies = []
    for piece in range(pieces):
        span = pl.ds(piece * width, width)
        copies.append(pltpu.make_async_copy(own_hbm.at[:, span], own_ref.at[:, span], arrived.at[piece]))
        copies[-1].start()
    for block in range(pixels // LANES):
        if block * LANES % width == 0:
            copies[block * LANES // width].wait()
        span = slice(block * LANES, (block + 1) * LANES)
        tile = jnp.concatenate([own_ref[:, span], other_ref[:, span]], axis=0)
        tile = tile.T
        wide_ref[span, :] = tile.astype(F32)
        out_ref[span, :LANES] = tile
    for column in range(BOX):
        out_ref[column * BOX:(column + 1) * BOX, LANES:] = wide_ref[
            pl.ds(column, BOX, stride=BOX), :
        ].astype(BF16)


def three_parts(value):
    high = value.astype(BF16).astype(F32)
    rest = value - high
    middle = rest.astype(BF16).astype(F32)
    return high, middle, (rest - middle).astype(BF16).astype(F32)


def slot_row(counts_ref, owners_ref, capacity):
    mic_count = counts_ref.shape[1]
    counts = [counts_ref[:, m:m + 1] for m in range(mic_count)]
    owners = [owners_ref[:, m:m + 1] for m in range(mic_count)]
    position = lax.broadcasted_iota(jnp.int32, (1, LANES), 1)
    slot = jnp.full((1, LANES), -1, jnp.int32)
    start = jnp.zeros((1, 1), jnp.int32)
    for mic in range(mic_count):
        before = jnp.zeros((1, 1), jnp.int32)
        for earlier in range(mic):
            before = before + jnp.where(owners[earlier] == owners[mic], counts[earlier], 0)
        stop = start + counts[mic]
        inside = (position >= start) & (position < stop)
        slot = jnp.where(inside, position + (owners[mic] * capacity + before - start), slot)
        start = stop
    return slot


def mirror_of_rows():
    row = lax.broadcasted_iota(jnp.int32, (LANES, LANES), 0)
    column = lax.broadcasted_iota(jnp.int32, (LANES, LANES), 1)
    return (column == (row // BOX) * BOX + (BOX - 1 - row % BOX)).astype(BF16)


def spans(pixels):
    return [slice(b * LANES, (b + 1) * LANES) for b in range(pixels // LANES)]


def score_kernel(capacity, counts_ref, owners_ref, first_ref, second_ref, own_ref, images_ref, scores_ref, stats_ref, flipped_ref):
    per_dev, pixels = own_ref.shape
    half = 2 * per_dev
    block_of = spans(pixels)
    second = jnp.where(lax.axis_index("rd") == 1, second_ref[...].astype(F32), own_ref[...].astype(F32))
    refs = jnp.concatenate([first_ref[...].astype(F32), second], axis=0)
    squares = jnp.sum(refs * refs, axis=1, keepdims=True)
    stacked = jnp.concatenate([refs[:, b] for b in block_of], axis=0)
    mirrored = jnp.dot(stacked.astype(BF16), mirror_of_rows(), preferred_element_type=F32)
    for b in range(len(block_of)):
        part = slice(b * half, (b + 1) * half)
        both = jnp.concatenate([stacked[part], mirrored[part]], axis=0)
        flipped_ref[:2 * half, block_of[b]] = both.astype(BF16)
        flipped_ref[2 * half:, block_of[-1 - b]] = rolled(both, BOX).astype(BF16)
    inner = jnp.dot(flipped_ref[...], images_ref[...], preferred_element_type=F32)
    scores = inner - 0.5 * jnp.concatenate([squares] * 4, axis=0)
    scores_ref[...] = scores
    highest = jnp.max(scores, axis=0, keepdims=True)
    highest = jnp.maximum(highest[:, :LANES], highest[:, LANES:])
    summed = jnp.sum(jnp.exp(scores - jnp.concatenate([highest, highest], axis=1)), axis=0, keepdims=True)
    summed = summed[:, :LANES] + summed[:, LANES:]
    slot = slot_row(counts_ref, owners_ref, capacity).astype(F32)
    stats_ref[...] = jnp.concatenate([highest, summed, slot, jnp.zeros((5, LANES), F32)], axis=0)


def weigh_kernel(scores_ref, stats_ref, other_stats_ref, images_ref, first_ref, second_ref, total_ref, kept_ref, sums_ref):
    per_dev = first_ref.shape[0]
    pixels = images_ref.shape[0]
    rows = LANES // 2
    half = 2 * per_dev
    block_of = spans(pixels)
    scores = scores_ref[...]
    other = rolled(other_stats_ref[...], BOX)
    highest = jnp.maximum(stats_ref[0:1], other[0:1])
    summed = stats_ref[1:2] * jnp.exp(stats_ref[0:1] - highest) + other[1:2] * jnp.exp(other[0:1] - highest)
    total = jnp.log(summed) + highest

    lane = lax.broadcasted_iota(jnp.int32, (1, LANES), 1)
    slot = jnp.where(lane < rows, stats_ref[2:3], other[2:3]).astype(jnp.int32)
    live = slot >= 0
    slot = jnp.where(live & (lane >= rows), slot + rows, slot)
    live = jnp.concatenate([live, live], axis=1)
    weights = jnp.where(live, jnp.exp(scores - jnp.concatenate([total, total], axis=1)), 0.0).astype(BF16)
    sums_ref[...] = lax.dot_general(
        weights, images_ref[...], (((1,), (1,)), ((), ())), preferred_element_type=F32
    )
    straight, swapped = [], []
    for b in range(len(block_of)):
        back = block_of[-1 - b]
        straight.append(sums_ref[0:half, block_of[b]] + rolled(sums_ref[2 * half:3 * half, back], BOX))
        swapped.append(sums_ref[half:2 * half, block_of[b]] + rolled(sums_ref[3 * half:, back], BOX))
    swapped = jnp.concatenate(swapped, axis=0)
    upper = swapped.astype(BF16)
    lower = (swapped - upper.astype(F32)).astype(BF16)
    mirror = mirror_of_rows()
    swapped = jnp.dot(upper, mirror, preferred_element_type=F32) + jnp.dot(
        lower, mirror, preferred_element_type=F32
    )
    for b in range(len(block_of)):
        both = straight[b] + swapped[b * half:(b + 1) * half]
        first_ref[:, block_of[b]] = both[:per_dev].astype(BF16)
        second_ref[:, block_of[b]] = both[per_dev:].astype(BF16)

    per_class = jnp.sum(weights.astype(F32), axis=1, keepdims=True)
    per_class = per_class[0:half] + per_class[half:2 * half] + per_class[2 * half:3 * half] + per_class[3 * half:]
    high, middle, low = three_parts(per_class)
    lanes = lax.broadcasted_iota(jnp.int32, (half, LANES), 1)
    sent = jnp.where(lanes == 0, high, jnp.where(lanes == 1, middle, jnp.where(lanes == 2, low, 0.0)))
    extra = slice(pixels, pixels + LANES)
    first_ref[:, extra] = sent[:per_dev].astype(BF16)
    second_ref[:, extra] = sent[per_dev:].astype(BF16)

    placing = (slot == lax.broadcasted_iota(jnp.int32, (LANES, LANES), 0)).astype(BF16)
    pieces = jnp.concatenate([*three_parts(total), jnp.zeros((5, LANES), F32)], axis=0)
    pieces = lax.dot_general(
        pieces.astype(BF16), placing, (((1,), (1,)), ((), ())), preferred_element_type=F32
    )
    total_ref[...] = pieces[0:1] + pieces[1:2] + pieces[2:3]
    last = slice(pixels + LANES, pixels + 2 * LANES)
    first_ref[:, last] = jnp.zeros((per_dev, LANES), BF16)
    second_ref[:, last] = pieces[:per_dev].astype(BF16)
    kept_ref[...] = second_ref[...]


def add_kernel(four_ref, two_ref, three_ref, one_ref, own_ref, out_ref):
    pixels = out_ref.shape[1] - LANES
    middle = jnp.where(lax.axis_index("rd") == 1, three_ref[:, :pixels].astype(F32), own_ref[:, :pixels].astype(F32))
    out_ref[:, :pixels] = (one_ref[:, :pixels].astype(F32) + two_ref[:, :pixels].astype(F32)) + (
        middle + four_ref[:, :pixels].astype(F32)
    )
    pieces = four_ref[:, pixels:].astype(F32)
    out_ref[:, pixels:] = jnp.broadcast_to(pieces[0:1] + pieces[1:2] + pieces[2:3], (out_ref.shape[0], LANES))


def finish_kernel(own_ref, other_ref, total_ref, means_hbm, weights_hbm, loglik_hbm,
                  means_ref, weights_ref, loglik_ref, sent):
    per_dev, pixels = means_ref.shape
    capacity = loglik_ref.shape[1] // 2
    extra = slice(pixels, pixels + LANES)
    last = slice(pixels + LANES, pixels + 2 * LANES)
    pieces = sent.shape[0] - 2
    width = pixels // pieces
    count = own_ref[:, extra] + other_ref[:, extra]
    count = count[:, 0:1] + count[:, 1:2] + count[:, 2:3]
    scale = 1.0 / (count + 1.0)
    copies = []
    for piece in range(pieces):
        span = pl.ds(piece * width, width)
        means_ref[:, span] = (own_ref[:, span] + other_ref[:, span]) * scale
        copies.append(pltpu.make_async_copy(means_ref.at[:, span], means_hbm.at[:, span], sent.at[piece]))
        copies[-1].start()
    across = lax.broadcasted_iota(jnp.int32, (per_dev, per_dev), 1)
    down = lax.broadcasted_iota(jnp.int32, (per_dev, per_dev), 0)
    weights_ref[...] = jnp.sum(jnp.where(across == down, count, 0.0), axis=0, keepdims=True)
    copies.append(pltpu.make_async_copy(weights_ref, weights_hbm, sent.at[pieces]))
    copies[-1].start()
    first = lax.axis_index("img") == 0
    arrived = jnp.where(
        lax.axis_index("rd") == 1, rolled(other_ref[0:1, last], 2 * capacity), own_ref[0:1, last]
    )
    arrived = jnp.where(first, arrived[:, :capacity], arrived[:, capacity:2 * capacity])
    mine = jnp.where(first, total_ref[:, :capacity], total_ref[:, capacity:2 * capacity])
    loglik_ref[:, :capacity] = jnp.where(first, mine, arrived)
    loglik_ref[:, capacity:] = jnp.where(first, arrived, mine)
    copies.append(pltpu.make_async_copy(loglik_ref, loglik_hbm, sent.at[pieces + 1]))
    copies[-1].start()
    for copy in copies:
        copy.wait()


def passed_along(array, axis, by):
    devices = lax.axis_size(axis)
    return lax.ppermute(array, axis, [(i, (i + by) % devices) for i in range(devices)])


def turn_image(field, turn_index):
    square = field.reshape(field.shape[:-1] + (BOX, BOX))
    if turn_index >= 4:
        square = jnp.flip(square, -1)
    square = jnp.rot90(square, turn_index % 4, axes=(-2, -1))
    return square.reshape(field.shape)


def turn_back(field, turn_index):
    square = field.reshape(field.shape[:-1] + (BOX, BOX))
    square = jnp.rot90(square, -(turn_index % 4), axes=(-2, -1))
    if turn_index >= 4:
        square = jnp.flip(square, -1)
    return square.reshape(field.shape)


def slot_table(count_row, owner_row, read_rows, capacity):
    mic_count = count_row.shape[0]
    ends = jnp.cumsum(count_row)
    position = jnp.arange(read_rows, dtype=jnp.int32)
    micrograph = jnp.sum((position[:, None] >= ends[None, :]).astype(jnp.int32), axis=1)
    usable = position < ends[mic_count - 1]
    matches = micrograph[:, None] == jnp.arange(mic_count, dtype=jnp.int32)[None, :]
    target = jnp.sum(jnp.where(matches, owner_row[None, :], 0), axis=1)
    earlier = (
        (target[:, None] == target[None, :])
        & usable[None, :]
        & (position[None, :] < position[:, None])
    )
    ranking = jnp.sum(earlier.astype(jnp.int32), axis=1)
    slot_index = jnp.where(usable, target * capacity + ranking, -1)
    placing = slot_index[None, :] == jnp.arange(read_rows, dtype=jnp.int32)[:, None]
    return (usable, placing)


def class_scores(particle_rows, piece):
    pixels = piece.shape[1]
    turned = jnp.stack(
        [turn_image(piece, turn_index) for turn_index in range(ROTS)], axis=1
    ).reshape(-1, pixels)
    squares = jnp.sum(piece.astype(jnp.float32) ** 2, axis=1)
    inner = lax.dot_general(
        particle_rows, turned, (((1,), (1,)), ((), ())), preferred_element_type=jnp.float32
    )
    return inner - 0.5 * jnp.repeat(squares, ROTS)[None, :]


def class_block(weights, particle_rows, first_class, class_count):
    chosen = lax.dynamic_slice_in_dim(weights, first_class * ROTS, class_count * ROTS, 1)
    summed = lax.dot_general(
        chosen, particle_rows, (((0,), (0,)), ((), ())), preferred_element_type=jnp.float32
    )
    summed = summed.reshape(class_count, ROTS, summed.shape[1])
    result = turn_back(summed[:, 0], 0)
    for turn_index in range(1, ROTS):
        result = result + turn_back(summed[:, turn_index], turn_index)
    return result


def local(images, counts, owners, references):
    read_rows, pixels = images.shape
    n_img = lax.axis_size("img")
    n_cls = lax.axis_size("cls")
    capacity = read_rows // n_img
    per_dev = references.shape[0]
    classes = per_dev * n_cls
    usable, placing = slot_table(counts[0], owners[0], read_rows, capacity)
    packed = jnp.dot(
        placing.astype(jnp.bfloat16), images, preferred_element_type=jnp.float32
    ).astype(jnp.bfloat16)
    filled = jnp.sum(placing.astype(jnp.float32), axis=1).astype(jnp.bfloat16)
    moved, arrived = (
        lax.all_to_all(
            packed.reshape(n_img, capacity, pixels), "img", split_axis=0, concat_axis=0, tiled=True
        ),
        lax.all_to_all(
            filled.reshape(n_img, capacity), "img", split_axis=0, concat_axis=0, tiled=True
        ),
    )
    particle_rows = moved.reshape(read_rows, pixels)
    live_rows = arrived.reshape(read_rows) > 0
    scores = class_scores(particle_rows, lax.all_gather(references, "cls", axis=0, tiled=True))
    highest = jnp.max(scores, axis=1, keepdims=True)
    total = jnp.log(jnp.sum(jnp.exp(scores - highest), axis=1, keepdims=True)) + highest
    weights = jnp.where(live_rows[:, None], jnp.exp(scores - total), 0.0).astype(jnp.bfloat16)
    row_loglik = jnp.where(live_rows, total[:, 0], 0.0)
    column_sums = jnp.sum(
        jnp.sum(weights.astype(jnp.float32), axis=0).reshape(classes, ROTS), axis=1
    )
    totals = lax.psum(column_sums, ("cls", "img", "rd"))
    device_index = lax.axis_index("cls")
    own_totals = lax.dynamic_slice_in_dim(totals, device_index * per_dev, per_dev)

    def cycle_stop(stop_index, carried):
        block = (device_index - 1 - stop_index) % n_cls
        carried = carried + class_block(weights, particle_rows, block * per_dev, per_dev)
        return passed_along(carried, "cls", 1)

    carried = lax.fori_loop(0, n_cls - 1, cycle_stop, jnp.zeros((per_dev, pixels), jnp.float32))
    class_sums = carried + class_block(weights, particle_rows, device_index * per_dev, per_dev)
    class_sums = lax.psum(class_sums, ("img", "rd"))
    class_means = class_sums / (own_totals[:, None] + 1.0)
    return (class_means, own_totals, row_loglik)


def swapped_by(array, by, axes=LINKED):
    devices = 1
    for axis in axes:
        devices = devices * lax.axis_size(axis)
    pairs = []
    for i in range(devices):
        step = by(i & 1) if callable(by) else by
        if step:
            pairs.append((i, i ^ step))
    return lax.ppermute(array, axes, pairs)


def call(kernel, outs, args, scalars=(), scratch=(), in_hbm=(), outs_in_hbm=False):
    specs = [
        pl.BlockSpec(memory_space=pltpu.SMEM if i in scalars else pltpu.HBM if i in in_hbm else pltpu.VMEM)
        for i in range(len(args))
    ]
    out_space = pltpu.HBM if outs_in_hbm else pltpu.VMEM
    return pl.pallas_call(
        kernel,
        out_shape=outs,
        in_specs=specs,
        out_specs=jax.tree.map(lambda _: pl.BlockSpec(memory_space=out_space), outs),
        scratch_shapes=list(scratch),
        compiler_params=pltpu.CompilerParams(vmem_limit_bytes=32 * 1024 * 1024),
    )(*args)


def direct(images, counts, owners, references):
    read_rows, pixels = images.shape
    capacity = read_rows // lax.axis_size("img")
    per_dev = references.shape[0]
    other_images = swapped_by(images, 1, ("rd",))
    ref_far = swapped_by(references, lambda rd: 8 if rd else 4)
    ref_near = swapped_by(references, lambda rd: 12 if rd else 2)
    shape = jax.ShapeDtypeStruct
    images = pltpu.with_memory_space_constraint(images, pltpu.HBM)
    turned = call(
        turn_kernel, shape((pixels, 2 * LANES), BF16), (images, other_images), (),
        [pltpu.VMEM((read_rows, pixels), BF16), pltpu.VMEM((pixels, LANES), F32), pltpu.SemaphoreType.DMA((2,))],
        in_hbm=(0,),
    )
    scores, stats = call(
        functools.partial(score_kernel, capacity),
        (shape((8 * per_dev, 2 * LANES), F32), shape((8, LANES), F32)),
        (counts, owners, ref_far, ref_near, references, turned), (),
        [pltpu.VMEM((8 * per_dev, pixels), BF16)],
    )
    other_stats = swapped_by(stats, 1, ("rd",))
    wide = pixels + 2 * LANES
    far, near, totals, kept = call(
        weigh_kernel,
        (shape((per_dev, wide), BF16), shape((per_dev, wide), BF16), shape((1, LANES), F32), shape((per_dev, wide), BF16)),
        (scores, stats, other_stats, turned), (), [pltpu.VMEM((8 * per_dev, pixels), F32)],
    )
    two = swapped_by(far, lambda rd: 10 if rd else 6)
    one = swapped_by(far, lambda rd: 8 if rd else 4)
    four = swapped_by(near, lambda rd: 14 if rd else 2)
    three = swapped_by(near, lambda rd: 12 if rd else 2)
    summed = call(add_kernel, shape((per_dev, wide), F32), (four, two, three, one, kept))
    other = swapped_by(summed, 1, ("rd",))
    outs = (shape((per_dev, pixels), F32), shape((1, per_dev), F32), shape((1, read_rows), F32))
    means, weights, loglik = call(
        finish_kernel, outs, (summed, other, totals), (),
        [pltpu.VMEM(out.shape, out.dtype) for out in outs] + [pltpu.SemaphoreType.DMA((6,))],
        outs_in_hbm=True,
    )
    return means, weights.reshape(per_dev), loglik.reshape(read_rows)


def solution(mesh):
    sizes = mesh.shape
    small = sizes["cls"] == 4 and sizes["img"] == 2 and sizes["rd"] == 2
    placed = (
        P(("groups", "cls", "img", "rd"), None),
        P(("groups", "cls", "img", "rd"), None),
        P(("groups", "cls", "img", "rd"), None),
        P(("groups", "cls"), None),
    )
    return jax.shard_map(
        direct if small else local,
        mesh=mesh,
        in_specs=placed,
        out_specs=(
            P(("groups", "cls"), None),
            P(("groups", "cls")),
            P(("groups", "cls", "img", "rd")),
        ),
        check_vma=False,
    )
```

```python
import functools

import jax
import jax.numpy as jnp
from jax import lax
from jax.experimental import pallas as pl
from jax.experimental.pallas import tpu as pltpu
from jax.sharding import PartitionSpec as P

BOX = 64
ROTS = 8
LANES = 128
PAIR = LANES // BOX
LINKED = ("cls", "img", "rd")
F32 = jnp.float32
BF16 = jnp.bfloat16


def rolled(tile, by):
    return jnp.concatenate([tile[:, by:], tile[:, :by]], axis=1)


def spans(pixels):
    return [slice(b * LANES, (b + 1) * LANES) for b in range(pixels // LANES)]


def slot_row(counts_ref, owners_ref, capacity):
    mic_count = counts_ref.shape[1]
    counts = [counts_ref[:, m:m + 1] for m in range(mic_count)]
    owners = [owners_ref[:, m:m + 1] for m in range(mic_count)]
    position = lax.broadcasted_iota(jnp.int32, (1, LANES), 1)
    slot = jnp.full((1, LANES), -1, jnp.int32)
    start = jnp.zeros((1, 1), jnp.int32)
    for mic in range(mic_count):
        before = jnp.zeros((1, 1), jnp.int32)
        for earlier in range(mic):
            before = before + jnp.where(owners[earlier] == owners[mic], counts[earlier], 0)
        stop = start + counts[mic]
        inside = (position >= start) & (position < stop)
        slot = jnp.where(inside, position + (owners[mic] * capacity + before - start), slot)
        start = stop
    return slot


def turn_kernel(capacity, own_hbm, counts_hbm, owners_hbm, classes_hbm, other_ref,
                out_ref, flat_ref, slots_ref, classes_ref, own_ref, counts_ref, owners_ref, arrived):
    pixels = other_ref.shape[1]
    pieces = arrived.shape[0] - 3
    width = pixels // pieces
    copies = []
    for piece in range(pieces):
        span = pl.ds(piece * width, width)
        copies.append(pltpu.make_async_copy(own_hbm.at[:, span], own_ref.at[:, span], arrived.at[piece]))
        copies[-1].start()
    small = [
        pltpu.make_async_copy(source, target, arrived.at[pieces + i])
        for i, (source, target) in enumerate(
            ((counts_hbm, counts_ref), (owners_hbm, owners_ref), (classes_hbm, classes_ref))
        )
    ]
    for copy in small:
        copy.start()
    for block, span in enumerate(spans(pixels)):
        if block * LANES % width == 0:
            copies[block * LANES // width].wait()
        tile = jnp.concatenate([own_ref[:, span], other_ref[:, span]], axis=0)
        flat_ref[:LANES, span] = tile
        out_ref[span, :LANES] = tile.T
    square = out_ref[:, :LANES].reshape(BOX, BOX, LANES)
    out_ref[:, LANES:] = jnp.swapaxes(square, 0, 1).reshape(pixels, LANES)
    for span in spans(pixels):
        flat_ref[LANES:, span] = out_ref[span, LANES:].T
    for copy in small:
        copy.wait()
    slot = slot_row(counts_ref, owners_ref, capacity).astype(F32)
    slots_ref[...] = jnp.broadcast_to(slot, slots_ref.shape)


def three_parts(value):
    high = value.astype(BF16).astype(F32)
    rest = value - high
    middle = rest.astype(BF16).astype(F32)
    return high, middle, (rest - middle).astype(BF16).astype(F32)


def mirror_of_rows():
    row = lax.broadcasted_iota(jnp.int32, (LANES, LANES), 0)
    column = lax.broadcasted_iota(jnp.int32, (LANES, LANES), 1)
    return (column == (row // BOX) * BOX + (BOX - 1 - row % BOX)).astype(BF16)


def score_kernel(slots_ref, two_ref, one_ref, own_ref, images_ref, scores_ref, sent_ref,
                 flipped_ref):
    per_dev, pixels = own_ref.shape
    half = 2 * per_dev
    block_of = spans(pixels)
    lead = lax.axis_index("rd") == 0
    two = two_ref[...].astype(F32)
    refs = jnp.concatenate(
        [jnp.where(lead, one_ref[...].astype(F32), two), jnp.where(lead, two, own_ref[...].astype(F32))], axis=0
    )
    squares = jnp.sum(refs * refs, axis=1, keepdims=True)
    stacked = jnp.concatenate([refs[:, b] for b in block_of], axis=0)
    mirrored = jnp.dot(stacked.astype(BF16), mirror_of_rows(), preferred_element_type=F32)
    for b in range(len(block_of)):
        part = slice(b * half, (b + 1) * half)
        both = jnp.concatenate([stacked[part], mirrored[part]], axis=0)
        flipped_ref[:2 * half, block_of[b]] = both.astype(BF16)
        flipped_ref[2 * half:, block_of[-1 - b]] = rolled(both, BOX).astype(BF16)
    inner = jnp.dot(flipped_ref[...], images_ref[...], preferred_element_type=F32)
    scores = inner - 0.5 * jnp.concatenate([squares] * 4, axis=0)
    scores_ref[...] = scores
    for f in range(4):
        sent_ref[f * per_dev:(f + 1) * per_dev] = scores[f * half + per_dev:(f + 1) * half]
    highest = jnp.max(scores, axis=0, keepdims=True)
    highest = jnp.maximum(highest[:, :LANES], highest[:, LANES:])
    summed = jnp.sum(jnp.exp(scores - jnp.concatenate([highest, highest], axis=1)), axis=0, keepdims=True)
    summed = summed[:, :LANES] + summed[:, LANES:]
    stats = jnp.concatenate([highest, summed, slots_ref[2:]], axis=0)
    sent_ref[4 * per_dev:] = jnp.concatenate([stats, stats], axis=1)


def weigh_kernel(scores_ref, sent_ref, arrived_ref, images_ref, first_ref, second_ref, total_ref, kept_ref, sums_ref):
    per_dev = first_ref.shape[0]
    pixels = images_ref.shape[1]
    rows = LANES // 2
    half = 2 * per_dev
    block_of = spans(pixels)
    top = 4 * per_dev
    stats = sent_ref[top:, :LANES]
    other = rolled(arrived_ref[top:, :LANES], BOX)
    arrived = jnp.concatenate(
        [rolled(arrived_ref[:top, :LANES], BOX), rolled(arrived_ref[:top, LANES:], BOX)], axis=1
    )
    scores = []
    for f in range(4):
        scores += [scores_ref[f * half:f * half + per_dev], arrived[f * per_dev:(f + 1) * per_dev]]
    scores = jnp.concatenate(scores, axis=0)
    highest = jnp.maximum(stats[0:1], other[0:1])
    summed = stats[1:2] * jnp.exp(stats[0:1] - highest) + other[1:2] * jnp.exp(other[0:1] - highest)
    total = jnp.log(summed) + highest

    lane = lax.broadcasted_iota(jnp.int32, (1, LANES), 1)
    slot = jnp.where(lane < rows, stats[2:3], other[2:3]).astype(jnp.int32)
    live = slot >= 0
    slot = jnp.where(live & (lane >= rows), slot + rows, slot)
    live = jnp.concatenate([live, live], axis=1)
    weights = jnp.where(live, jnp.exp(scores - jnp.concatenate([total, total], axis=1)), 0.0).astype(BF16)
    sums_ref[...] = jnp.dot(weights, images_ref[...], preferred_element_type=F32)
    straight, swapped = [], []
    for b in range(len(block_of)):
        back = block_of[-1 - b]
        straight.append(sums_ref[0:half, block_of[b]] + rolled(sums_ref[2 * half:3 * half, back], BOX))
        swapped.append(sums_ref[half:2 * half, block_of[b]] + rolled(sums_ref[3 * half:, back], BOX))
    swapped = jnp.concatenate(swapped, axis=0)
    upper = swapped.astype(BF16)
    lower = (swapped - upper.astype(F32)).astype(BF16)
    mirror = mirror_of_rows()
    swapped = jnp.dot(upper, mirror, preferred_element_type=F32) + jnp.dot(
        lower, mirror, preferred_element_type=F32
    )
    for b in range(len(block_of)):
        both = straight[b] + swapped[b * half:(b + 1) * half]
        first_ref[:, block_of[b]] = both[:per_dev].astype(BF16)
        second_ref[:, block_of[b]] = both[per_dev:].astype(BF16)

    per_class = jnp.sum(weights.astype(F32), axis=1, keepdims=True)
    per_class = per_class[0:half] + per_class[half:2 * half] + per_class[2 * half:3 * half] + per_class[3 * half:]
    high, middle, low = three_parts(per_class)
    lanes = lax.broadcasted_iota(jnp.int32, (half, LANES), 1)
    sent = jnp.where(lanes == 0, high, jnp.where(lanes == 1, middle, jnp.where(lanes == 2, low, 0.0)))
    extra = slice(pixels, pixels + LANES)
    first_ref[:, extra] = sent[:per_dev].astype(BF16)
    second_ref[:, extra] = sent[per_dev:].astype(BF16)

    placing = (slot == lax.broadcasted_iota(jnp.int32, (LANES, LANES), 0)).astype(BF16)
    pieces = jnp.concatenate([*three_parts(total), jnp.zeros((5, LANES), F32)], axis=0)
    pieces = lax.dot_general(
        pieces.astype(BF16), placing, (((1,), (1,)), ((), ())), preferred_element_type=F32
    )
    total_ref[...] = pieces[0:1] + pieces[1:2] + pieces[2:3]
    last = slice(pixels + LANES, pixels + 2 * LANES)
    first_ref[:, last] = jnp.zeros((per_dev, LANES), BF16)
    second_ref[:, last] = pieces[:per_dev].astype(BF16)
    kept_ref[...] = second_ref[...]


def add_kernel(two_ref, four_ref, one_ref, three_ref, own_ref, out_ref):
    pixels = out_ref.shape[1] - LANES
    middle = jnp.where(lax.axis_index("rd") == 1, three_ref[:, :pixels].astype(F32), own_ref[:, :pixels].astype(F32))
    out_ref[:, :pixels] = (one_ref[:, :pixels].astype(F32) + two_ref[:, :pixels].astype(F32)) + (
        middle + four_ref[:, :pixels].astype(F32)
    )
    pieces = four_ref[:, pixels:].astype(F32)
    out_ref[:, pixels:] = jnp.broadcast_to(pieces[0:1] + pieces[1:2] + pieces[2:3], (out_ref.shape[0], LANES))


def finish_kernel(own_ref, other_ref, total_ref, means_hbm, weights_hbm, loglik_hbm,
                  means_ref, weights_ref, loglik_ref, sent):
    per_dev, pixels = means_ref.shape
    capacity = loglik_ref.shape[1] // 2
    extra = slice(pixels, pixels + LANES)
    last = slice(pixels + LANES, pixels + 2 * LANES)
    pieces = sent.shape[0] - 2
    width = pixels // pieces
    count = own_ref[:, extra] + other_ref[:, extra]
    count = count[:, 0:1] + count[:, 1:2] + count[:, 2:3]
    scale = 1.0 / (count + 1.0)
    copies = []
    for piece in range(pieces):
        span = pl.ds(piece * width, width)
        means_ref[:, span] = (own_ref[:, span] + other_ref[:, span]) * scale
        copies.append(pltpu.make_async_copy(means_ref.at[:, span], means_hbm.at[:, span], sent.at[piece]))
        copies[-1].start()
    across = lax.broadcasted_iota(jnp.int32, (per_dev, per_dev), 1)
    down = lax.broadcasted_iota(jnp.int32, (per_dev, per_dev), 0)
    weights_ref[...] = jnp.sum(jnp.where(across == down, count, 0.0), axis=0, keepdims=True)
    copies.append(pltpu.make_async_copy(weights_ref, weights_hbm, sent.at[pieces]))
    copies[-1].start()
    first = lax.axis_index("img") == 0
    arrived = jnp.where(
        lax.axis_index("rd") == 1, rolled(other_ref[0:1, last], 2 * capacity), own_ref[0:1, last]
    )
    arrived = jnp.where(first, arrived[:, :capacity], arrived[:, capacity:2 * capacity])
    mine = jnp.where(first, total_ref[:, :capacity], total_ref[:, capacity:2 * capacity])
    loglik_ref[:, :capacity] = jnp.where(first, mine, arrived)
    loglik_ref[:, capacity:] = jnp.where(first, arrived, mine)
    copies.append(pltpu.make_async_copy(loglik_ref, loglik_hbm, sent.at[pieces + 1]))
    copies[-1].start()
    for copy in copies:
        copy.wait()


def passed_along(array, axis, by):
    devices = lax.axis_size(axis)
    return lax.ppermute(array, axis, [(i, (i + by) % devices) for i in range(devices)])


def turn_image(field, turn_index):
    square = field.reshape(field.shape[:-1] + (BOX, BOX))
    if turn_index >= 4:
        square = jnp.flip(square, -1)
    square = jnp.rot90(square, turn_index % 4, axes=(-2, -1))
    return square.reshape(field.shape)


def turn_back(field, turn_index):
    square = field.reshape(field.shape[:-1] + (BOX, BOX))
    square = jnp.rot90(square, -(turn_index % 4), axes=(-2, -1))
    if turn_index >= 4:
        square = jnp.flip(square, -1)
    return square.reshape(field.shape)


def slot_table(count_row, owner_row, read_rows, capacity):
    mic_count = count_row.shape[0]
    ends = jnp.cumsum(count_row)
    position = jnp.arange(read_rows, dtype=jnp.int32)
    micrograph = jnp.sum((position[:, None] >= ends[None, :]).astype(jnp.int32), axis=1)
    usable = position < ends[mic_count - 1]
    matches = micrograph[:, None] == jnp.arange(mic_count, dtype=jnp.int32)[None, :]
    target = jnp.sum(jnp.where(matches, owner_row[None, :], 0), axis=1)
    earlier = (
        (target[:, None] == target[None, :])
        & usable[None, :]
        & (position[None, :] < position[:, None])
    )
    ranking = jnp.sum(earlier.astype(jnp.int32), axis=1)
    slot_index = jnp.where(usable, target * capacity + ranking, -1)
    placing = slot_index[None, :] == jnp.arange(read_rows, dtype=jnp.int32)[:, None]
    return (usable, placing)


def class_scores(particle_rows, piece):
    pixels = piece.shape[1]
    turned = jnp.stack(
        [turn_image(piece, turn_index) for turn_index in range(ROTS)], axis=1
    ).reshape(-1, pixels)
    squares = jnp.sum(piece.astype(jnp.float32) ** 2, axis=1)
    inner = lax.dot_general(
        particle_rows, turned, (((1,), (1,)), ((), ())), preferred_element_type=jnp.float32
    )
    return inner - 0.5 * jnp.repeat(squares, ROTS)[None, :]


def class_block(weights, particle_rows, first_class, class_count):
    chosen = lax.dynamic_slice_in_dim(weights, first_class * ROTS, class_count * ROTS, 1)
    summed = lax.dot_general(
        chosen, particle_rows, (((0,), (0,)), ((), ())), preferred_element_type=jnp.float32
    )
    summed = summed.reshape(class_count, ROTS, summed.shape[1])
    result = turn_back(summed[:, 0], 0)
    for turn_index in range(1, ROTS):
        result = result + turn_back(summed[:, turn_index], turn_index)
    return result


def local(images, counts, owners, references):
    read_rows, pixels = images.shape
    n_img = lax.axis_size("img")
    n_cls = lax.axis_size("cls")
    capacity = read_rows // n_img
    per_dev = references.shape[0]
    classes = per_dev * n_cls
    usable, placing = slot_table(counts[0], owners[0], read_rows, capacity)
    packed = jnp.dot(
        placing.astype(jnp.bfloat16), images, preferred_element_type=jnp.float32
    ).astype(jnp.bfloat16)
    filled = jnp.sum(placing.astype(jnp.float32), axis=1).astype(jnp.bfloat16)
    moved, arrived = (
        lax.all_to_all(
            packed.reshape(n_img, capacity, pixels), "img", split_axis=0, concat_axis=0, tiled=True
        ),
        lax.all_to_all(
            filled.reshape(n_img, capacity), "img", split_axis=0, concat_axis=0, tiled=True
        ),
    )
    particle_rows = moved.reshape(read_rows, pixels)
    live_rows = arrived.reshape(read_rows) > 0
    scores = class_scores(particle_rows, lax.all_gather(references, "cls", axis=0, tiled=True))
    highest = jnp.max(scores, axis=1, keepdims=True)
    total = jnp.log(jnp.sum(jnp.exp(scores - highest), axis=1, keepdims=True)) + highest
    weights = jnp.where(live_rows[:, None], jnp.exp(scores - total), 0.0).astype(jnp.bfloat16)
    row_loglik = jnp.where(live_rows, total[:, 0], 0.0)
    column_sums = jnp.sum(
        jnp.sum(weights.astype(jnp.float32), axis=0).reshape(classes, ROTS), axis=1
    )
    totals = lax.psum(column_sums, ("cls", "img", "rd"))
    device_index = lax.axis_index("cls")
    own_totals = lax.dynamic_slice_in_dim(totals, device_index * per_dev, per_dev)

    def cycle_stop(stop_index, carried):
        block = (device_index - 1 - stop_index) % n_cls
        carried = carried + class_block(weights, particle_rows, block * per_dev, per_dev)
        return passed_along(carried, "cls", 1)

    carried = lax.fori_loop(0, n_cls - 1, cycle_stop, jnp.zeros((per_dev, pixels), jnp.float32))
    class_sums = carried + class_block(weights, particle_rows, device_index * per_dev, per_dev)
    class_sums = lax.psum(class_sums, ("img", "rd"))
    class_means = class_sums / (own_totals[:, None] + 1.0)
    return (class_means, own_totals, row_loglik)


def swapped_by(array, by, axes=LINKED):
    devices = 1
    for axis in axes:
        devices = devices * lax.axis_size(axis)
    pairs = []
    for i in range(devices):
        step = by(i & 1) if callable(by) else by
        if step:
            pairs.append((i, i ^ step))
    return lax.ppermute(array, axes, pairs)


def call(kernel, outs, args, scalars=(), scratch=(), in_hbm=(), outs_in_hbm=False):
    specs = [
        pl.BlockSpec(memory_space=pltpu.SMEM if i in scalars else pltpu.HBM if i in in_hbm else pltpu.VMEM)
        for i in range(len(args))
    ]
    out_space = pltpu.HBM if outs_in_hbm else pltpu.VMEM
    return pl.pallas_call(
        kernel,
        out_shape=outs,
        in_specs=specs,
        out_specs=jax.tree.map(lambda _: pl.BlockSpec(memory_space=out_space), outs),
        scratch_shapes=list(scratch),
        compiler_params=pltpu.CompilerParams(vmem_limit_bytes=16 * 1024 * 1024),
    )(*args)


def direct(images, counts, owners, references):
    read_rows, pixels = images.shape
    capacity = read_rows // lax.axis_size("img")
    per_dev = references.shape[0]
    other_images = swapped_by(images, 1, ("rd",))
    ref_one = swapped_by(references, 4)
    ref_two = swapped_by(references, lambda rd: 12 if rd else 8)
    shape = jax.ShapeDtypeStruct
    in_hbm = [pltpu.with_memory_space_constraint(x, pltpu.HBM) for x in (images, counts, owners, references)]
    turned, flat, slots, classes = call(
        functools.partial(turn_kernel, capacity),
        (shape((pixels, 2 * LANES), BF16), shape((2 * LANES, pixels), BF16), shape((8, LANES), F32),
         shape(references.shape, BF16)),
        (*in_hbm, other_images), (),
        [pltpu.VMEM((read_rows, pixels), BF16), pltpu.VMEM(counts.shape, jnp.int32),
         pltpu.VMEM(owners.shape, jnp.int32), pltpu.SemaphoreType.DMA((5,))],
        in_hbm=(0, 1, 2, 3),
    )
    scores, sent = call(
        score_kernel,
        (shape((8 * per_dev, 2 * LANES), F32), shape((4 * per_dev + 8, 2 * LANES), F32)),
        (slots, ref_two, ref_one, classes, turned), (),
        [pltpu.VMEM((8 * per_dev, pixels), BF16)],
    )
    arrived = swapped_by(sent, 1, ("rd",))
    wide = pixels + 2 * LANES
    far, near, totals, kept = call(
        weigh_kernel,
        (shape((per_dev, wide), BF16), shape((per_dev, wide), BF16), shape((1, LANES), F32), shape((per_dev, wide), BF16)),
        (scores, sent, arrived, flat), (), [pltpu.VMEM((8 * per_dev, pixels), F32)],
    )
    two = swapped_by(far, lambda rd: 14 if rd else 6)
    one = swapped_by(far, lambda rd: 12 if rd else 4)
    four = swapped_by(near, lambda rd: 10 if rd else 2)
    three = swapped_by(near, lambda rd: 8 if rd else 2)
    summed = call(add_kernel, shape((per_dev, wide), F32), (two, four, one, three, kept))
    other = swapped_by(summed, 1, ("rd",))
    outs = (shape((per_dev, pixels), F32), shape((1, per_dev), F32), shape((1, read_rows), F32))
    means, weights, loglik = call(
        finish_kernel, outs, (summed, other, totals), (),
        [pltpu.VMEM(out.shape, out.dtype) for out in outs] + [pltpu.SemaphoreType.DMA((6,))],
        outs_in_hbm=True,
    )
    return means, weights.reshape(per_dev), loglik.reshape(read_rows)


def solution(mesh):
    sizes = mesh.shape
    small = sizes["cls"] == 4 and sizes["img"] == 2 and sizes["rd"] == 2
    placed = (
        P(("groups", "cls", "img", "rd"), None),
        P(("groups", "cls", "img", "rd"), None),
        P(("groups", "cls", "img", "rd"), None),
        P(("groups", "cls"), None),
    )
    return jax.shard_map(
        direct if small else local,
        mesh=mesh,
        in_specs=placed,
        out_specs=(
            P(("groups", "cls"), None),
            P(("groups", "cls")),
            P(("groups", "cls", "img", "rd")),
        ),
        check_vma=False,
    )
```

```python
import functools

import jax
import jax.numpy as jnp
from jax import lax
from jax.experimental import pallas as pl
from jax.experimental.pallas import tpu as pltpu
from jax.sharding import PartitionSpec as P

BOX = 64
ROTS = 8
LANES = 128
PAIR = LANES // BOX
LINKED = ("cls", "img", "rd")
F32 = jnp.float32
BF16 = jnp.bfloat16


def rolled(tile, by):
    return jnp.concatenate([tile[:, by:], tile[:, :by]], axis=1)


def spans(pixels):
    return [slice(b * LANES, (b + 1) * LANES) for b in range(pixels // LANES)]


def slot_row(counts_ref, owners_ref, capacity):
    mic_count = counts_ref.shape[1]
    counts = [counts_ref[:, m:m + 1] for m in range(mic_count)]
    owners = [owners_ref[:, m:m + 1] for m in range(mic_count)]
    position = lax.broadcasted_iota(jnp.int32, (1, LANES), 1)
    slot = jnp.full((1, LANES), -1, jnp.int32)
    start = jnp.zeros((1, 1), jnp.int32)
    for mic in range(mic_count):
        before = jnp.zeros((1, 1), jnp.int32)
        for earlier in range(mic):
            before = before + jnp.where(owners[earlier] == owners[mic], counts[earlier], 0)
        stop = start + counts[mic]
        inside = (position >= start) & (position < stop)
        slot = jnp.where(inside, position + (owners[mic] * capacity + before - start), slot)
        start = stop
    return slot


def turn_kernel(capacity, own_hbm, counts_hbm, owners_hbm, classes_hbm, other_ref,
                out_ref, flat_ref, slots_ref, classes_ref, own_ref, counts_ref, owners_ref, arrived):
    pixels = other_ref.shape[1]
    pieces = arrived.shape[0] - 3
    width = pixels // pieces
    copies = []
    for piece in range(pieces):
        span = pl.ds(piece * width, width)
        copies.append(pltpu.make_async_copy(own_hbm.at[:, span], own_ref.at[:, span], arrived.at[piece]))
        copies[-1].start()
    small = [
        pltpu.make_async_copy(source, target, arrived.at[pieces + i])
        for i, (source, target) in enumerate(
            ((counts_hbm, counts_ref), (owners_hbm, owners_ref), (classes_hbm, classes_ref))
        )
    ]
    for copy in small:
        copy.start()
    for block, span in enumerate(spans(pixels)):
        if block * LANES % width == 0:
            copies[block * LANES // width].wait()
        tile = jnp.concatenate([own_ref[:, span], other_ref[:, span]], axis=0)
        flat_ref[:LANES, span] = tile
        out_ref[span, :LANES] = tile.T
    square = out_ref[:, :LANES].reshape(BOX, BOX, LANES)
    out_ref[:, LANES:] = jnp.swapaxes(square, 0, 1).reshape(pixels, LANES)
    for span in spans(pixels):
        flat_ref[LANES:, span] = out_ref[span, LANES:].T
    for copy in small:
        copy.wait()
    slot = slot_row(counts_ref, owners_ref, capacity).astype(F32)
    slots_ref[...] = jnp.broadcast_to(slot, slots_ref.shape)


def three_parts(value):
    high = value.astype(BF16).astype(F32)
    rest = value - high
    middle = rest.astype(BF16).astype(F32)
    return high, middle, (rest - middle).astype(BF16).astype(F32)


def mirror_of_rows():
    row = lax.broadcasted_iota(jnp.int32, (LANES, LANES), 0)
    column = lax.broadcasted_iota(jnp.int32, (LANES, LANES), 1)
    return (column == (row // BOX) * BOX + (BOX - 1 - row % BOX)).astype(BF16)


def score_kernel(slots_ref, two_ref, one_ref, own_ref, images_ref, scores_ref, sent_ref,
                 flipped_ref):
    per_dev, pixels = own_ref.shape
    half = 2 * per_dev
    block_of = spans(pixels)
    lead = lax.axis_index("rd") == 0
    two = two_ref[...].astype(F32)
    refs = jnp.concatenate(
        [jnp.where(lead, own_ref[...].astype(F32), two), jnp.where(lead, two, one_ref[...].astype(F32))], axis=0
    )
    squares = jnp.sum(refs * refs, axis=1, keepdims=True)
    stacked = jnp.concatenate([refs[:, b] for b in block_of], axis=0)
    mirrored = jnp.dot(stacked.astype(BF16), mirror_of_rows(), preferred_element_type=F32)
    for b in range(len(block_of)):
        part = slice(b * half, (b + 1) * half)
        both = jnp.concatenate([stacked[part], mirrored[part]], axis=0)
        flipped_ref[:2 * half, block_of[b]] = both.astype(BF16)
        flipped_ref[2 * half:, block_of[-1 - b]] = rolled(both, BOX).astype(BF16)
    inner = jnp.dot(flipped_ref[...], images_ref[...], preferred_element_type=F32)
    scores = inner - 0.5 * jnp.concatenate([squares] * 4, axis=0)
    scores_ref[...] = scores
    for f in range(4):
        sent_ref[f * per_dev:(f + 1) * per_dev] = scores[f * half + per_dev:(f + 1) * half]
    highest = jnp.max(scores, axis=0, keepdims=True)
    highest = jnp.maximum(highest[:, :LANES], highest[:, LANES:])
    summed = jnp.sum(jnp.exp(scores - jnp.concatenate([highest, highest], axis=1)), axis=0, keepdims=True)
    summed = summed[:, :LANES] + summed[:, LANES:]
    stats = jnp.concatenate([highest, summed, slots_ref[2:]], axis=0)
    sent_ref[4 * per_dev:] = jnp.concatenate([stats, stats], axis=1)


def weigh_kernel(scores_ref, sent_ref, arrived_ref, images_ref, first_ref, second_ref, total_ref, kept_ref, sums_ref):
    per_dev = first_ref.shape[0]
    pixels = images_ref.shape[1]
    rows = LANES // 2
    half = 2 * per_dev
    block_of = spans(pixels)
    top = 4 * per_dev
    stats = sent_ref[top:, :LANES]
    other = rolled(arrived_ref[top:, :LANES], BOX)
    arrived = jnp.concatenate(
        [rolled(arrived_ref[:top, :LANES], BOX), rolled(arrived_ref[:top, LANES:], BOX)], axis=1
    )
    lead = lax.axis_index("rd") == 0
    scores = []
    for f in range(4):
        here, there = scores_ref[f * half:f * half + per_dev], arrived[f * per_dev:(f + 1) * per_dev]
        scores += [jnp.where(lead, there, here), jnp.where(lead, here, there)]
    scores = jnp.concatenate(scores, axis=0)
    highest = jnp.maximum(stats[0:1], other[0:1])
    summed = stats[1:2] * jnp.exp(stats[0:1] - highest) + other[1:2] * jnp.exp(other[0:1] - highest)
    total = jnp.log(summed) + highest

    lane = lax.broadcasted_iota(jnp.int32, (1, LANES), 1)
    slot = jnp.where(lane < rows, stats[2:3], other[2:3]).astype(jnp.int32)
    live = slot >= 0
    slot = jnp.where(live & (lane >= rows), slot + rows, slot)
    live = jnp.concatenate([live, live], axis=1)
    weights = jnp.where(live, jnp.exp(scores - jnp.concatenate([total, total], axis=1)), 0.0).astype(BF16)
    sums_ref[...] = jnp.dot(weights, images_ref[...], preferred_element_type=F32)
    straight, swapped = [], []
    for b in range(len(block_of)):
        back = block_of[-1 - b]
        straight.append(sums_ref[0:half, block_of[b]] + rolled(sums_ref[2 * half:3 * half, back], BOX))
        swapped.append(sums_ref[half:2 * half, block_of[b]] + rolled(sums_ref[3 * half:, back], BOX))
    swapped = jnp.concatenate(swapped, axis=0)
    upper = swapped.astype(BF16)
    lower = (swapped - upper.astype(F32)).astype(BF16)
    mirror = mirror_of_rows()
    swapped = jnp.dot(upper, mirror, preferred_element_type=F32) + jnp.dot(
        lower, mirror, preferred_element_type=F32
    )
    for b in range(len(block_of)):
        both = straight[b] + swapped[b * half:(b + 1) * half]
        first_ref[:, block_of[b]] = both[:per_dev].astype(BF16)
        second_ref[:, block_of[b]] = both[per_dev:].astype(BF16)

    per_class = jnp.sum(weights.astype(F32), axis=1, keepdims=True)
    per_class = per_class[0:half] + per_class[half:2 * half] + per_class[2 * half:3 * half] + per_class[3 * half:]
    high, middle, low = three_parts(per_class)
    lanes = lax.broadcasted_iota(jnp.int32, (half, LANES), 1)
    sent = jnp.where(lanes == 0, high, jnp.where(lanes == 1, middle, jnp.where(lanes == 2, low, 0.0)))
    extra = slice(pixels, pixels + LANES)
    first_ref[:, extra] = sent[:per_dev].astype(BF16)
    second_ref[:, extra] = sent[per_dev:].astype(BF16)

    placing = (slot == lax.broadcasted_iota(jnp.int32, (LANES, LANES), 0)).astype(BF16)
    pieces = jnp.concatenate([*three_parts(total), jnp.zeros((5, LANES), F32)], axis=0)
    pieces = lax.dot_general(
        pieces.astype(BF16), placing, (((1,), (1,)), ((), ())), preferred_element_type=F32
    )
    total_ref[...] = pieces[0:1] + pieces[1:2] + pieces[2:3]
    last = slice(pixels + LANES, pixels + 2 * LANES)
    first_ref[:, last] = jnp.zeros((per_dev, LANES), BF16)
    second_ref[:, last] = pieces[:per_dev].astype(BF16)
    kept_ref[...] = second_ref[...]


def add_kernel(two_ref, four_ref, one_ref, three_ref, own_ref, out_ref):
    pixels = out_ref.shape[1] - LANES
    middle = jnp.where(lax.axis_index("rd") == 1, three_ref[:, :pixels].astype(F32), own_ref[:, :pixels].astype(F32))
    out_ref[:, :pixels] = (one_ref[:, :pixels].astype(F32) + two_ref[:, :pixels].astype(F32)) + (
        middle + four_ref[:, :pixels].astype(F32)
    )
    pieces = four_ref[:, pixels:].astype(F32)
    out_ref[:, pixels:] = jnp.broadcast_to(pieces[0:1] + pieces[1:2] + pieces[2:3], (out_ref.shape[0], LANES))


def finish_kernel(own_ref, other_ref, total_ref, means_hbm, weights_hbm, loglik_hbm,
                  means_ref, weights_ref, loglik_ref, sent):
    per_dev, pixels = means_ref.shape
    capacity = loglik_ref.shape[1] // 2
    extra = slice(pixels, pixels + LANES)
    last = slice(pixels + LANES, pixels + 2 * LANES)
    pieces = sent.shape[0] - 2
    width = pixels // pieces
    count = own_ref[:, extra] + other_ref[:, extra]
    count = count[:, 0:1] + count[:, 1:2] + count[:, 2:3]
    divisor = count + 1.0
    copies = []
    for piece in range(pieces):
        span = pl.ds(piece * width, width)
        means_ref[:, span] = (own_ref[:, span] + other_ref[:, span]) / divisor
        copies.append(pltpu.make_async_copy(means_ref.at[:, span], means_hbm.at[:, span], sent.at[piece]))
        copies[-1].start()
    across = lax.broadcasted_iota(jnp.int32, (per_dev, per_dev), 1)
    down = lax.broadcasted_iota(jnp.int32, (per_dev, per_dev), 0)
    weights_ref[...] = jnp.sum(jnp.where(across == down, count, 0.0), axis=0, keepdims=True)
    copies.append(pltpu.make_async_copy(weights_ref, weights_hbm, sent.at[pieces]))
    copies[-1].start()
    first = lax.axis_index("img") == 0
    arrived = jnp.where(
        lax.axis_index("rd") == 1, rolled(other_ref[0:1, last], 2 * capacity), own_ref[0:1, last]
    )
    arrived = jnp.where(first, arrived[:, :capacity], arrived[:, capacity:2 * capacity])
    mine = jnp.where(first, total_ref[:, :capacity], total_ref[:, capacity:2 * capacity])
    loglik_ref[:, :capacity] = jnp.where(first, mine, arrived)
    loglik_ref[:, capacity:] = jnp.where(first, arrived, mine)
    copies.append(pltpu.make_async_copy(loglik_ref, loglik_hbm, sent.at[pieces + 1]))
    copies[-1].start()
    for copy in copies:
        copy.wait()


def passed_along(array, axis, by):
    devices = lax.axis_size(axis)
    return lax.ppermute(array, axis, [(i, (i + by) % devices) for i in range(devices)])


def turn_image(field, turn_index):
    square = field.reshape(field.shape[:-1] + (BOX, BOX))
    if turn_index >= 4:
        square = jnp.flip(square, -1)
    square = jnp.rot90(square, turn_index % 4, axes=(-2, -1))
    return square.reshape(field.shape)


def turn_back(field, turn_index):
    square = field.reshape(field.shape[:-1] + (BOX, BOX))
    square = jnp.rot90(square, -(turn_index % 4), axes=(-2, -1))
    if turn_index >= 4:
        square = jnp.flip(square, -1)
    return square.reshape(field.shape)


def slot_table(count_row, owner_row, read_rows, capacity):
    mic_count = count_row.shape[0]
    ends = jnp.cumsum(count_row)
    position = jnp.arange(read_rows, dtype=jnp.int32)
    micrograph = jnp.sum((position[:, None] >= ends[None, :]).astype(jnp.int32), axis=1)
    usable = position < ends[mic_count - 1]
    matches = micrograph[:, None] == jnp.arange(mic_count, dtype=jnp.int32)[None, :]
    target = jnp.sum(jnp.where(matches, owner_row[None, :], 0), axis=1)
    earlier = (
        (target[:, None] == target[None, :])
        & usable[None, :]
        & (position[None, :] < position[:, None])
    )
    ranking = jnp.sum(earlier.astype(jnp.int32), axis=1)
    slot_index = jnp.where(usable, target * capacity + ranking, -1)
    placing = slot_index[None, :] == jnp.arange(read_rows, dtype=jnp.int32)[:, None]
    return (usable, placing)


def class_scores(particle_rows, piece):
    pixels = piece.shape[1]
    turned = jnp.stack(
        [turn_image(piece, turn_index) for turn_index in range(ROTS)], axis=1
    ).reshape(-1, pixels)
    squares = jnp.sum(piece.astype(jnp.float32) ** 2, axis=1)
    inner = lax.dot_general(
        particle_rows, turned, (((1,), (1,)), ((), ())), preferred_element_type=jnp.float32
    )
    return inner - 0.5 * jnp.repeat(squares, ROTS)[None, :]


def class_block(weights, particle_rows, first_class, class_count):
    chosen = lax.dynamic_slice_in_dim(weights, first_class * ROTS, class_count * ROTS, 1)
    summed = lax.dot_general(
        chosen, particle_rows, (((0,), (0,)), ((), ())), preferred_element_type=jnp.float32
    )
    summed = summed.reshape(class_count, ROTS, summed.shape[1])
    result = turn_back(summed[:, 0], 0)
    for turn_index in range(1, ROTS):
        result = result + turn_back(summed[:, turn_index], turn_index)
    return result


def local(images, counts, owners, references):
    read_rows, pixels = images.shape
    n_img = lax.axis_size("img")
    n_cls = lax.axis_size("cls")
    capacity = read_rows // n_img
    per_dev = references.shape[0]
    classes = per_dev * n_cls
    usable, placing = slot_table(counts[0], owners[0], read_rows, capacity)
    packed = jnp.dot(
        placing.astype(jnp.bfloat16), images, preferred_element_type=jnp.float32
    ).astype(jnp.bfloat16)
    filled = jnp.sum(placing.astype(jnp.float32), axis=1).astype(jnp.bfloat16)
    moved, arrived = (
        lax.all_to_all(
            packed.reshape(n_img, capacity, pixels), "img", split_axis=0, concat_axis=0, tiled=True
        ),
        lax.all_to_all(
            filled.reshape(n_img, capacity), "img", split_axis=0, concat_axis=0, tiled=True
        ),
    )
    particle_rows = moved.reshape(read_rows, pixels)
    live_rows = arrived.reshape(read_rows) > 0
    scores = class_scores(particle_rows, lax.all_gather(references, "cls", axis=0, tiled=True))
    highest = jnp.max(scores, axis=1, keepdims=True)
    total = jnp.log(jnp.sum(jnp.exp(scores - highest), axis=1, keepdims=True)) + highest
    weights = jnp.where(live_rows[:, None], jnp.exp(scores - total), 0.0).astype(jnp.bfloat16)
    row_loglik = jnp.where(live_rows, total[:, 0], 0.0)
    column_sums = jnp.sum(
        jnp.sum(weights.astype(jnp.float32), axis=0).reshape(classes, ROTS), axis=1
    )
    totals = lax.psum(column_sums, ("cls", "img", "rd"))
    device_index = lax.axis_index("cls")
    own_totals = lax.dynamic_slice_in_dim(totals, device_index * per_dev, per_dev)

    def cycle_stop(stop_index, carried):
        block = (device_index - 1 - stop_index) % n_cls
        carried = carried + class_block(weights, particle_rows, block * per_dev, per_dev)
        return passed_along(carried, "cls", 1)

    carried = lax.fori_loop(0, n_cls - 1, cycle_stop, jnp.zeros((per_dev, pixels), jnp.float32))
    class_sums = carried + class_block(weights, particle_rows, device_index * per_dev, per_dev)
    class_sums = lax.psum(class_sums, ("img", "rd"))
    class_means = class_sums / (own_totals[:, None] + 1.0)
    return (class_means, own_totals, row_loglik)


def swapped_by(array, by, axes=LINKED):
    devices = 1
    for axis in axes:
        devices = devices * lax.axis_size(axis)
    pairs = []
    for i in range(devices):
        step = by(i) if callable(by) else by
        if step:
            pairs.append((i, i ^ step))
    return lax.ppermute(array, axes, pairs)


def call(kernel, outs, args, scalars=(), scratch=(), in_hbm=(), outs_in_hbm=False):
    specs = [
        pl.BlockSpec(memory_space=pltpu.SMEM if i in scalars else pltpu.HBM if i in in_hbm else pltpu.VMEM)
        for i in range(len(args))
    ]
    out_space = pltpu.HBM if outs_in_hbm else pltpu.VMEM
    return pl.pallas_call(
        kernel,
        out_shape=outs,
        in_specs=specs,
        out_specs=jax.tree.map(lambda _: pl.BlockSpec(memory_space=out_space), outs),
        scratch_shapes=list(scratch),
        compiler_params=pltpu.CompilerParams(vmem_limit_bytes=16 * 1024 * 1024),
    )(*args)


def direct(images, counts, owners, references):
    read_rows, pixels = images.shape
    capacity = read_rows // lax.axis_size("img")
    per_dev = references.shape[0]
    other_images = swapped_by(images, 1, ("rd",))
    ref_one = swapped_by(references, lambda i: 4 if i & 1 else 2)
    ref_two = swapped_by(references, lambda i: (12 if i & 1 else 8) if (i >> 2) in (0, 3) else (9 if i & 1 else 13))
    shape = jax.ShapeDtypeStruct
    in_hbm = [pltpu.with_memory_space_constraint(x, pltpu.HBM) for x in (images, counts, owners, references)]
    turned, flat, slots, classes = call(
        functools.partial(turn_kernel, capacity),
        (shape((pixels, 2 * LANES), BF16), shape((2 * LANES, pixels), BF16), shape((8, LANES), F32),
         shape(references.shape, BF16)),
        (*in_hbm, other_images), (),
        [pltpu.VMEM((read_rows, pixels), BF16), pltpu.VMEM(counts.shape, jnp.int32),
         pltpu.VMEM(owners.shape, jnp.int32), pltpu.SemaphoreType.DMA((5,))],
        in_hbm=(0, 1, 2, 3),
    )
    scores, sent = call(
        score_kernel,
        (shape((8 * per_dev, 2 * LANES), F32), shape((4 * per_dev + 8, 2 * LANES), F32)),
        (slots, ref_two, ref_one, classes, turned), (),
        [pltpu.VMEM((8 * per_dev, pixels), BF16)],
    )
    arrived = swapped_by(sent, 1, ("rd",))
    wide = pixels + 2 * LANES
    far, near, totals, kept = call(
        weigh_kernel,
        (shape((per_dev, wide), BF16), shape((per_dev, wide), BF16), shape((1, LANES), F32), shape((per_dev, wide), BF16)),
        (scores, sent, arrived, flat), (), [pltpu.VMEM((8 * per_dev, pixels), F32)],
    )
    two = swapped_by(far, lambda i: 14 if i & 1 else 6)
    one = swapped_by(far, lambda i: 12 if i & 1 else 4)
    four = swapped_by(near, lambda i: 10 if i & 1 else 2)
    three = swapped_by(near, lambda i: 8 if i & 1 else 2)
    summed = call(add_kernel, shape((per_dev, wide), F32), (two, four, one, three, kept))
    other = swapped_by(summed, 1, ("rd",))
    outs = (shape((per_dev, pixels), F32), shape((1, per_dev), F32), shape((1, read_rows), F32))
    means, weights, loglik = call(
        finish_kernel, outs, (summed, other, totals), (),
        [pltpu.VMEM(out.shape, out.dtype) for out in outs] + [pltpu.SemaphoreType.DMA((6,))],
        outs_in_hbm=True,
    )
    return means, weights.reshape(per_dev), loglik.reshape(read_rows)


def solution(mesh):
    sizes = mesh.shape
    small = sizes["cls"] == 4 and sizes["img"] == 2 and sizes["rd"] == 2
    placed = (
        P(("groups", "cls", "img", "rd"), None),
        P(("groups", "cls", "img", "rd"), None),
        P(("groups", "cls", "img", "rd"), None),
        P(("groups", "cls"), None),
    )
    return jax.shard_map(
        direct if small else local,
        mesh=mesh,
        in_specs=placed,
        out_specs=(
            P(("groups", "cls"), None),
            P(("groups", "cls")),
            P(("groups", "cls", "img", "rd")),
        ),
        check_vma=False,
    )
```

```python
import functools

import jax
import jax.numpy as jnp
from jax import lax
from jax.experimental import pallas as pl
from jax.experimental.pallas import tpu as pltpu
from jax.sharding import PartitionSpec as P

BOX = 64
ROTS = 8
LANES = 128
PAIR = LANES // BOX
LINKED = ("cls", "img", "rd")
F32 = jnp.float32
BF16 = jnp.bfloat16


def rolled(tile, by):
    return jnp.concatenate([tile[:, by:], tile[:, :by]], axis=1)


def spans(pixels):
    return [slice(b * LANES, (b + 1) * LANES) for b in range(pixels // LANES)]


def slot_row(counts_ref, owners_ref, capacity):
    mic_count = counts_ref.shape[1]
    counts = [counts_ref[:, m:m + 1] for m in range(mic_count)]
    owners = [owners_ref[:, m:m + 1] for m in range(mic_count)]
    position = lax.broadcasted_iota(jnp.int32, (1, LANES), 1)
    slot = jnp.full((1, LANES), -1, jnp.int32)
    start = jnp.zeros((1, 1), jnp.int32)
    for mic in range(mic_count):
        before = jnp.zeros((1, 1), jnp.int32)
        for earlier in range(mic):
            before = before + jnp.where(owners[earlier] == owners[mic], counts[earlier], 0)
        stop = start + counts[mic]
        inside = (position >= start) & (position < stop)
        slot = jnp.where(inside, position + (owners[mic] * capacity + before - start), slot)
        start = stop
    return slot


def turn_kernel(capacity, own_hbm, counts_hbm, owners_hbm, classes_hbm, other_ref,
                out_ref, flat_ref, slots_ref, classes_ref, counts_ref, owners_ref, arrived):
    pixels = other_ref.shape[1]
    pieces = arrived.shape[0] - 3
    width = pixels // pieces
    copies = []
    for piece in range(pieces):
        span = pl.ds(piece * width, width)
        copies.append(pltpu.make_async_copy(own_hbm.at[:, span], flat_ref.at[pl.ds(0, other_ref.shape[0]), span], arrived.at[piece]))
        copies[-1].start()
    small = [
        pltpu.make_async_copy(source, target, arrived.at[pieces + i])
        for i, (source, target) in enumerate(
            ((counts_hbm, counts_ref), (owners_hbm, owners_ref), (classes_hbm, classes_ref))
        )
    ]
    for copy in small:
        copy.start()
    for block, span in enumerate(spans(pixels)):
        if block * LANES % width == 0:
            copies[block * LANES // width].wait()
        flat_ref[other_ref.shape[0]:LANES, span] = other_ref[:, span]
        tile = flat_ref[:LANES, span]
        out_ref[span, :LANES] = tile.T
    square = out_ref[:, :LANES].reshape(BOX, BOX, LANES)
    out_ref[:, LANES:] = jnp.swapaxes(square, 0, 1).reshape(pixels, LANES)
    for span in spans(pixels):
        flat_ref[LANES:, span] = out_ref[span, LANES:].T
    for copy in small:
        copy.wait()
    slot = slot_row(counts_ref, owners_ref, capacity).astype(F32)
    slots_ref[...] = jnp.broadcast_to(slot, slots_ref.shape)


def three_parts(value):
    high = value.astype(BF16).astype(F32)
    rest = value - high
    middle = rest.astype(BF16).astype(F32)
    return high, middle, (rest - middle).astype(BF16).astype(F32)


def leads():
    place = lax.axis_index("cls")
    inner = ((place == 1) | (place == 2)).astype(jnp.int32)
    return lax.axis_index("rd") == inner


def mirror_of_rows():
    row = lax.broadcasted_iota(jnp.int32, (LANES, LANES), 0)
    column = lax.broadcasted_iota(jnp.int32, (LANES, LANES), 1)
    return (column == (row // BOX) * BOX + (BOX - 1 - row % BOX)).astype(BF16)


def score_kernel(slots_ref, two_ref, one_ref, own_ref, images_ref, scores_ref, sent_ref,
                 flipped_ref):
    per_dev, pixels = own_ref.shape
    half = 2 * per_dev
    block_of = spans(pixels)
    swapped_block = jnp.where(leads(), one_ref[...].astype(F32), own_ref[...].astype(F32))
    refs = jnp.concatenate([two_ref[...].astype(F32), swapped_block], axis=0)
    squares = jnp.sum(refs * refs, axis=1, keepdims=True)
    stacked = jnp.concatenate([refs[:, b] for b in block_of], axis=0)
    mirrored = jnp.dot(stacked.astype(BF16), mirror_of_rows(), preferred_element_type=F32)
    for b in range(len(block_of)):
        part = slice(b * half, (b + 1) * half)
        both = jnp.concatenate([stacked[part], mirrored[part]], axis=0)
        flipped_ref[:2 * half, block_of[b]] = both.astype(BF16)
        flipped_ref[2 * half:, block_of[-1 - b]] = rolled(both, BOX).astype(BF16)
    inner = jnp.dot(flipped_ref[...], images_ref[...], preferred_element_type=F32)
    scores = inner - 0.5 * jnp.concatenate([squares] * 4, axis=0)
    scores_ref[...] = scores
    for f in range(4):
        sent_ref[f * per_dev:(f + 1) * per_dev] = scores[f * half + per_dev:(f + 1) * half]
    highest = jnp.max(scores, axis=0, keepdims=True)
    highest = jnp.maximum(highest[:, :LANES], highest[:, LANES:])
    summed = jnp.sum(jnp.exp(scores - jnp.concatenate([highest, highest], axis=1)), axis=0, keepdims=True)
    summed = summed[:, :LANES] + summed[:, LANES:]
    stats = jnp.concatenate([highest, summed, slots_ref[2:]], axis=0)
    sent_ref[4 * per_dev:] = jnp.concatenate([stats, stats], axis=1)


def weigh_kernel(scores_ref, sent_ref, arrived_ref, images_ref, first_ref, second_ref, total_ref, kept_ref, sums_ref):
    per_dev = first_ref.shape[0]
    pixels = images_ref.shape[1]
    rows = LANES // 2
    half = 2 * per_dev
    block_of = spans(pixels)
    top = 4 * per_dev
    stats = sent_ref[top:, :LANES]
    other = rolled(arrived_ref[top:, :LANES], BOX)
    arrived = jnp.concatenate(
        [rolled(arrived_ref[:top, :LANES], BOX), rolled(arrived_ref[:top, LANES:], BOX)], axis=1
    )
    lead = leads()
    scores = []
    for f in range(4):
        here, there = scores_ref[f * half:f * half + per_dev], arrived[f * per_dev:(f + 1) * per_dev]
        scores += [jnp.where(lead, there, here), jnp.where(lead, here, there)]
    scores = jnp.concatenate(scores, axis=0)
    highest = jnp.maximum(stats[0:1], other[0:1])
    summed = stats[1:2] * jnp.exp(stats[0:1] - highest) + other[1:2] * jnp.exp(other[0:1] - highest)
    total = jnp.log(summed) + highest

    lane = lax.broadcasted_iota(jnp.int32, (1, LANES), 1)
    slot = jnp.where(lane < rows, stats[2:3], other[2:3]).astype(jnp.int32)
    live = slot >= 0
    slot = jnp.where(live & (lane >= rows), slot + rows, slot)
    live = jnp.concatenate([live, live], axis=1)
    weights = jnp.where(live, jnp.exp(scores - jnp.concatenate([total, total], axis=1)), 0.0).astype(BF16)
    sums_ref[...] = jnp.dot(weights, images_ref[...], preferred_element_type=F32)
    straight, swapped = [], []
    for b in range(len(block_of)):
        back = block_of[-1 - b]
        straight.append(sums_ref[0:half, block_of[b]] + rolled(sums_ref[2 * half:3 * half, back], BOX))
        swapped.append(sums_ref[half:2 * half, block_of[b]] + rolled(sums_ref[3 * half:, back], BOX))
    swapped = jnp.concatenate(swapped, axis=0)
    upper = swapped.astype(BF16)
    lower = (swapped - upper.astype(F32)).astype(BF16)
    mirror = mirror_of_rows()
    swapped = jnp.dot(upper, mirror, preferred_element_type=F32) + jnp.dot(
        lower, mirror, preferred_element_type=F32
    )
    for b in range(len(block_of)):
        both = straight[b] + swapped[b * half:(b + 1) * half]
        first_ref[:, block_of[b]] = both[:per_dev].astype(BF16)
        second_ref[:, block_of[b]] = both[per_dev:].astype(BF16)

    per_class = jnp.sum(weights.astype(F32), axis=1, keepdims=True)
    per_class = per_class[0:half] + per_class[half:2 * half] + per_class[2 * half:3 * half] + per_class[3 * half:]
    high, middle, low = three_parts(per_class)
    lanes = lax.broadcasted_iota(jnp.int32, (half, LANES), 1)
    sent = jnp.where(lanes == 0, high, jnp.where(lanes == 1, middle, jnp.where(lanes == 2, low, 0.0)))
    extra = slice(pixels, pixels + LANES)
    first_ref[:, extra] = sent[:per_dev].astype(BF16)
    second_ref[:, extra] = sent[per_dev:].astype(BF16)

    placing = (slot == lax.broadcasted_iota(jnp.int32, (LANES, LANES), 0)).astype(BF16)
    pieces = jnp.concatenate([*three_parts(total), jnp.zeros((5, LANES), F32)], axis=0)
    pieces = lax.dot_general(
        pieces.astype(BF16), placing, (((1,), (1,)), ((), ())), preferred_element_type=F32
    )
    total_ref[...] = pieces[0:1] + pieces[1:2] + pieces[2:3]
    last = slice(pixels + LANES, pixels + 2 * LANES)
    first_ref[:, last] = pieces[:per_dev].astype(BF16)
    second_ref[:, last] = jnp.zeros((per_dev, LANES), BF16)
    kept_ref[...] = first_ref[...]


def add_kernel(pd_ref, qx_ref, po_ref, qx1_ref, kept_ref, out_ref):
    pixels = out_ref.shape[1] - LANES
    own = jnp.where(leads(), kept_ref[:, :pixels].astype(F32), pd_ref[:, :pixels].astype(F32))
    out_ref[:, :pixels] = (qx_ref[:, :pixels].astype(F32) + qx1_ref[:, :pixels].astype(F32)) + (
        own + po_ref[:, :pixels].astype(F32)
    )
    pieces = po_ref[:, pixels:].astype(F32)
    out_ref[:, pixels:] = jnp.broadcast_to(pieces[0:1] + pieces[1:2] + pieces[2:3], (out_ref.shape[0], LANES))


def finish_kernel(own_ref, other_ref, total_ref, means_hbm, weights_hbm, loglik_hbm,
                  means_ref, weights_ref, loglik_ref, sent):
    per_dev, pixels = means_ref.shape
    capacity = loglik_ref.shape[1] // 2
    extra = slice(pixels, pixels + LANES)
    last = slice(pixels + LANES, pixels + 2 * LANES)
    pieces = sent.shape[0] - 2
    width = pixels // pieces
    count = own_ref[:, extra] + other_ref[:, extra]
    count = count[:, 0:1] + count[:, 1:2] + count[:, 2:3]
    divisor = count + 1.0
    copies = []
    for piece in range(pieces):
        span = pl.ds(piece * width, width)
        means_ref[:, span] = (own_ref[:, span] + other_ref[:, span]) / divisor
        copies.append(pltpu.make_async_copy(means_ref.at[:, span], means_hbm.at[:, span], sent.at[piece]))
        copies[-1].start()
    across = lax.broadcasted_iota(jnp.int32, (per_dev, per_dev), 1)
    down = lax.broadcasted_iota(jnp.int32, (per_dev, per_dev), 0)
    weights_ref[...] = jnp.sum(jnp.where(across == down, count, 0.0), axis=0, keepdims=True)
    copies.append(pltpu.make_async_copy(weights_ref, weights_hbm, sent.at[pieces]))
    copies[-1].start()
    first = lax.axis_index("img") == 0
    arrived = jnp.where(leads(), own_ref[0:1, last], rolled(other_ref[0:1, last], 2 * capacity))
    arrived = jnp.where(first, arrived[:, :capacity], arrived[:, capacity:2 * capacity])
    mine = jnp.where(first, total_ref[:, :capacity], total_ref[:, capacity:2 * capacity])
    loglik_ref[:, :capacity] = jnp.where(first, mine, arrived)
    loglik_ref[:, capacity:] = jnp.where(first, arrived, mine)
    copies.append(pltpu.make_async_copy(loglik_ref, loglik_hbm, sent.at[pieces + 1]))
    copies[-1].start()
    for copy in copies:
        copy.wait()


def passed_along(array, axis, by):
    devices = lax.axis_size(axis)
    return lax.ppermute(array, axis, [(i, (i + by) % devices) for i in range(devices)])


def turn_image(field, turn_index):
    square = field.reshape(field.shape[:-1] + (BOX, BOX))
    if turn_index >= 4:
        square = jnp.flip(square, -1)
    square = jnp.rot90(square, turn_index % 4, axes=(-2, -1))
    return square.reshape(field.shape)


def turn_back(field, turn_index):
    square = field.reshape(field.shape[:-1] + (BOX, BOX))
    square = jnp.rot90(square, -(turn_index % 4), axes=(-2, -1))
    if turn_index >= 4:
        square = jnp.flip(square, -1)
    return square.reshape(field.shape)


def slot_table(count_row, owner_row, read_rows, capacity):
    mic_count = count_row.shape[0]
    ends = jnp.cumsum(count_row)
    position = jnp.arange(read_rows, dtype=jnp.int32)
    micrograph = jnp.sum((position[:, None] >= ends[None, :]).astype(jnp.int32), axis=1)
    usable = position < ends[mic_count - 1]
    matches = micrograph[:, None] == jnp.arange(mic_count, dtype=jnp.int32)[None, :]
    target = jnp.sum(jnp.where(matches, owner_row[None, :], 0), axis=1)
    earlier = (
        (target[:, None] == target[None, :])
        & usable[None, :]
        & (position[None, :] < position[:, None])
    )
    ranking = jnp.sum(earlier.astype(jnp.int32), axis=1)
    slot_index = jnp.where(usable, target * capacity + ranking, -1)
    placing = slot_index[None, :] == jnp.arange(read_rows, dtype=jnp.int32)[:, None]
    return (usable, placing)


def class_scores(particle_rows, piece):
    pixels = piece.shape[1]
    turned = jnp.stack(
        [turn_image(piece, turn_index) for turn_index in range(ROTS)], axis=1
    ).reshape(-1, pixels)
    squares = jnp.sum(piece.astype(jnp.float32) ** 2, axis=1)
    inner = lax.dot_general(
        particle_rows, turned, (((1,), (1,)), ((), ())), preferred_element_type=jnp.float32
    )
    return inner - 0.5 * jnp.repeat(squares, ROTS)[None, :]


def class_block(weights, particle_rows, first_class, class_count):
    chosen = lax.dynamic_slice_in_dim(weights, first_class * ROTS, class_count * ROTS, 1)
    summed = lax.dot_general(
        chosen, particle_rows, (((0,), (0,)), ((), ())), preferred_element_type=jnp.float32
    )
    summed = summed.reshape(class_count, ROTS, summed.shape[1])
    result = turn_back(summed[:, 0], 0)
    for turn_index in range(1, ROTS):
        result = result + turn_back(summed[:, turn_index], turn_index)
    return result


def local(images, counts, owners, references):
    read_rows, pixels = images.shape
    n_img = lax.axis_size("img")
    n_cls = lax.axis_size("cls")
    capacity = read_rows // n_img
    per_dev = references.shape[0]
    classes = per_dev * n_cls
    usable, placing = slot_table(counts[0], owners[0], read_rows, capacity)
    packed = jnp.dot(
        placing.astype(jnp.bfloat16), images, preferred_element_type=jnp.float32
    ).astype(jnp.bfloat16)
    filled = jnp.sum(placing.astype(jnp.float32), axis=1).astype(jnp.bfloat16)
    moved, arrived = (
        lax.all_to_all(
            packed.reshape(n_img, capacity, pixels), "img", split_axis=0, concat_axis=0, tiled=True
        ),
        lax.all_to_all(
            filled.reshape(n_img, capacity), "img", split_axis=0, concat_axis=0, tiled=True
        ),
    )
    particle_rows = moved.reshape(read_rows, pixels)
    live_rows = arrived.reshape(read_rows) > 0
    scores = class_scores(particle_rows, lax.all_gather(references, "cls", axis=0, tiled=True))
    highest = jnp.max(scores, axis=1, keepdims=True)
    total = jnp.log(jnp.sum(jnp.exp(scores - highest), axis=1, keepdims=True)) + highest
    weights = jnp.where(live_rows[:, None], jnp.exp(scores - total), 0.0).astype(jnp.bfloat16)
    row_loglik = jnp.where(live_rows, total[:, 0], 0.0)
    column_sums = jnp.sum(
        jnp.sum(weights.astype(jnp.float32), axis=0).reshape(classes, ROTS), axis=1
    )
    totals = lax.psum(column_sums, ("cls", "img", "rd"))
    device_index = lax.axis_index("cls")
    own_totals = lax.dynamic_slice_in_dim(totals, device_index * per_dev, per_dev)

    def cycle_stop(stop_index, carried):
        block = (device_index - 1 - stop_index) % n_cls
        carried = carried + class_block(weights, particle_rows, block * per_dev, per_dev)
        return passed_along(carried, "cls", 1)

    carried = lax.fori_loop(0, n_cls - 1, cycle_stop, jnp.zeros((per_dev, pixels), jnp.float32))
    class_sums = carried + class_block(weights, particle_rows, device_index * per_dev, per_dev)
    class_sums = lax.psum(class_sums, ("img", "rd"))
    class_means = class_sums / (own_totals[:, None] + 1.0)
    return (class_means, own_totals, row_loglik)


def swapped(array):
    return lax.ppermute(array, "rd", [(0, 1), (1, 0)])


def traded(array, steps):
    pairs = []
    for source in range(16):
        role = (source & 1) ^ (source >> 2 in (1, 2))
        target = (source & ~1) ^ steps[role]
        pairs.append((source, target | (role ^ (target >> 2 in (1, 2)))))
    return lax.ppermute(array, LINKED, pairs)


def call(kernel, outs, args, scalars=(), scratch=(), in_hbm=(), outs_in_hbm=False):
    specs = [
        pl.BlockSpec(memory_space=pltpu.SMEM if i in scalars else pltpu.HBM if i in in_hbm else pltpu.VMEM)
        for i in range(len(args))
    ]
    out_space = pltpu.HBM if outs_in_hbm else pltpu.VMEM
    return pl.pallas_call(
        kernel,
        out_shape=outs,
        in_specs=specs,
        out_specs=jax.tree.map(lambda _: pl.BlockSpec(memory_space=out_space), outs),
        scratch_shapes=list(scratch),
        compiler_params=pltpu.CompilerParams(vmem_limit_bytes=16 * 1024 * 1024),
    )(*args)


def direct(images, counts, owners, references):
    read_rows, pixels = images.shape
    if 2 * read_rows != LANES:
        return local(images, counts, owners, references)
    capacity = read_rows // lax.axis_size("img")
    per_dev = references.shape[0]
    other_images = swapped(images)
    ref_one = traded(references, (4, 2))
    ref_two = traded(references, (8, 12))
    shape = jax.ShapeDtypeStruct
    in_hbm = [pltpu.with_memory_space_constraint(x, pltpu.HBM) for x in (images, counts, owners, references)]
    turned, flat, slots, classes = call(
        functools.partial(turn_kernel, capacity),
        (shape((pixels, 2 * LANES), BF16), shape((2 * LANES, pixels), BF16), shape((8, LANES), F32),
         shape(references.shape, BF16)),
        (*in_hbm, other_images), (),
        [pltpu.VMEM(counts.shape, jnp.int32),
         pltpu.VMEM(owners.shape, jnp.int32), pltpu.SemaphoreType.DMA((5,))],
        in_hbm=(0, 1, 2, 3),
    )
    scores, sent = call(
        score_kernel,
        (shape((8 * per_dev, 2 * LANES), F32), shape((4 * per_dev + 8, 2 * LANES), F32)),
        (slots, ref_two, ref_one, classes, turned), (),
        [pltpu.VMEM((8 * per_dev, pixels), BF16)],
    )
    arrived = swapped(sent)
    wide = pixels + 2 * LANES
    first, second, totals, kept = call(
        weigh_kernel,
        (shape((per_dev, wide), BF16), shape((per_dev, wide), BF16), shape((1, LANES), F32), shape((per_dev, wide), BF16)),
        (scores, sent, arrived, flat), (), [pltpu.VMEM((8 * per_dev, pixels), F32)],
    )
    po = traded(first, (2, 12))
    pd = traded(first, (2, 14))
    qx1 = traded(second, (10, 4))
    qx = traded(second, (8, 6))
    summed = call(add_kernel, shape((per_dev, wide), F32), (pd, qx, po, qx1, kept))
    other = swapped(summed)
    outs = (shape((per_dev, pixels), F32), shape((1, per_dev), F32), shape((1, read_rows), F32))
    means, weights, loglik = call(
        finish_kernel, outs, (summed, other, totals), (),
        [pltpu.VMEM(out.shape, out.dtype) for out in outs] + [pltpu.SemaphoreType.DMA((6,))],
        outs_in_hbm=True,
    )
    return means, weights.reshape(per_dev), loglik.reshape(read_rows)


def solution(mesh):
    sizes = mesh.shape
    small = sizes["cls"] == 4 and sizes["img"] == 2 and sizes["rd"] == 2
    placed = (
        P(("groups", "cls", "img", "rd"), None),
        P(("groups", "cls", "img", "rd"), None),
        P(("groups", "cls", "img", "rd"), None),
        P(("groups", "cls"), None),
    )
    return jax.shard_map(
        direct if small else local,
        mesh=mesh,
        in_specs=placed,
        out_specs=(
            P(("groups", "cls"), None),
            P(("groups", "cls")),
            P(("groups", "cls", "img", "rd")),
        ),
        check_vma=False,
    )
```

```python
import functools

import jax
import jax.numpy as jnp
from jax import lax
from jax.experimental import pallas as pl
from jax.experimental.pallas import tpu as pltpu
from jax.sharding import PartitionSpec as P

BOX = 64
ROTS = 8
LANES = 128
PAIR = LANES // BOX
LINKED = ("cls", "img", "rd")
F32 = jnp.float32
BF16 = jnp.bfloat16


def rolled(tile, by):
    if tile.shape[1] == LANES and by == BOX:
        return pltpu.roll(tile, BOX, 1)
    return jnp.concatenate([tile[:, by:], tile[:, :by]], axis=1)


def spans(pixels):
    return [slice(b * LANES, (b + 1) * LANES) for b in range(pixels // LANES)]


def slot_row(counts_ref, owners_ref, capacity):
    mic_count = counts_ref.shape[1]
    counts = [counts_ref[:, m:m + 1] for m in range(mic_count)]
    owners = [owners_ref[:, m:m + 1] for m in range(mic_count)]
    position = lax.broadcasted_iota(jnp.int32, (1, LANES), 1)
    slot = jnp.full((1, LANES), -1, jnp.int32)
    start = jnp.zeros((1, 1), jnp.int32)
    for mic in range(mic_count):
        before = jnp.zeros((1, 1), jnp.int32)
        for earlier in range(mic):
            before = before + jnp.where(owners[earlier] == owners[mic], counts[earlier], 0)
        stop = start + counts[mic]
        inside = (position >= start) & (position < stop)
        slot = jnp.where(inside, position + (owners[mic] * capacity + before - start), slot)
        start = stop
    return slot


def turn_kernel(capacity, own_hbm, counts_hbm, owners_hbm, classes_hbm, other_ref,
                out_ref, flat_ref, slots_ref, classes_ref, counts_ref, owners_ref, arrived):
    pixels = other_ref.shape[1]
    pieces = arrived.shape[0] - 3
    width = pixels // pieces
    copies = []
    for piece in range(pieces):
        span = pl.ds(piece * width, width)
        copies.append(pltpu.make_async_copy(own_hbm.at[:, span], flat_ref.at[pl.ds(0, other_ref.shape[0]), span], arrived.at[piece]))
        copies[-1].start()
    small = [
        pltpu.make_async_copy(source, target, arrived.at[pieces + i])
        for i, (source, target) in enumerate(
            ((counts_hbm, counts_ref), (owners_hbm, owners_ref), (classes_hbm, classes_ref))
        )
    ]
    for copy in small:
        copy.start()
    for block, span in enumerate(spans(pixels)):
        if block * LANES % width == 0:
            copies[block * LANES // width].wait()
        flat_ref[other_ref.shape[0]:LANES, span] = other_ref[:, span]
        tile = flat_ref[:LANES, span]
        out_ref[span, :LANES] = tile.T
    square = out_ref[:, :LANES].reshape(BOX, BOX, LANES)
    out_ref[:, LANES:] = jnp.swapaxes(square, 0, 1).reshape(pixels, LANES)
    for span in spans(pixels):
        flat_ref[LANES:, span] = out_ref[span, LANES:].T
    for copy in small:
        copy.wait()
    slot = slot_row(counts_ref, owners_ref, capacity).astype(F32)
    slots_ref[...] = jnp.broadcast_to(slot, slots_ref.shape)


def three_parts(value):
    high = value.astype(BF16).astype(F32)
    rest = value - high
    middle = rest.astype(BF16).astype(F32)
    return high, middle, (rest - middle).astype(BF16).astype(F32)


def leads():
    place = lax.axis_index("cls")
    inner = ((place == 1) | (place == 2)).astype(jnp.int32)
    return lax.axis_index("rd") == inner


def mirror_of_rows():
    row = lax.broadcasted_iota(jnp.int32, (LANES, LANES), 0)
    column = lax.broadcasted_iota(jnp.int32, (LANES, LANES), 1)
    return (column == (row // BOX) * BOX + (BOX - 1 - row % BOX)).astype(BF16)


def score_kernel(slots_ref, two_ref, one_ref, own_ref, images_ref, scores_ref, sent_ref,
                 flipped_ref):
    per_dev, pixels = own_ref.shape
    half = 2 * per_dev
    block_of = spans(pixels)
    swapped_block = jnp.where(leads(), one_ref[...].astype(F32), own_ref[...].astype(F32))
    refs = jnp.concatenate([two_ref[...].astype(F32), swapped_block], axis=0)
    squares = jnp.sum(refs * refs, axis=1, keepdims=True)
    stacked = jnp.concatenate([refs[:, b] for b in block_of], axis=0)
    mirrored = jnp.dot(stacked.astype(BF16), mirror_of_rows(), preferred_element_type=F32)
    for b in range(len(block_of)):
        part = slice(b * half, (b + 1) * half)
        both = jnp.concatenate([stacked[part], mirrored[part]], axis=0)
        flipped_ref[:2 * half, block_of[b]] = both.astype(BF16)
        flipped_ref[2 * half:, block_of[-1 - b]] = rolled(both, BOX).astype(BF16)
    inner = jnp.dot(flipped_ref[...], images_ref[...], preferred_element_type=F32)
    scores = inner - 0.5 * jnp.concatenate([squares] * 4, axis=0)
    scores_ref[...] = scores
    for f in range(4):
        sent_ref[f * per_dev:(f + 1) * per_dev] = scores[f * half + per_dev:(f + 1) * half]
    highest = jnp.max(scores, axis=0, keepdims=True)
    highest = jnp.maximum(highest[:, :LANES], highest[:, LANES:])
    summed = jnp.sum(jnp.exp(scores - jnp.concatenate([highest, highest], axis=1)), axis=0, keepdims=True)
    summed = summed[:, :LANES] + summed[:, LANES:]
    stats = jnp.concatenate([highest, summed, slots_ref[2:]], axis=0)
    sent_ref[4 * per_dev:] = jnp.concatenate([stats, stats], axis=1)


def weigh_kernel(scores_ref, sent_ref, arrived_ref, images_ref, first_ref, second_ref, total_ref, kept_ref, sums_ref):
    per_dev = first_ref.shape[0]
    pixels = images_ref.shape[1]
    rows = LANES // 2
    half = 2 * per_dev
    block_of = spans(pixels)
    top = 4 * per_dev
    stats = sent_ref[top:, :LANES]
    other = rolled(arrived_ref[top:, :LANES], BOX)
    arrived = jnp.concatenate(
        [rolled(arrived_ref[:top, :LANES], BOX), rolled(arrived_ref[:top, LANES:], BOX)], axis=1
    )
    lead = leads()
    scores = []
    for f in range(4):
        here, there = scores_ref[f * half:f * half + per_dev], arrived[f * per_dev:(f + 1) * per_dev]
        scores += [jnp.where(lead, there, here), jnp.where(lead, here, there)]
    scores = jnp.concatenate(scores, axis=0)
    highest = jnp.maximum(stats[0:1], other[0:1])
    summed = stats[1:2] * jnp.exp(stats[0:1] - highest) + other[1:2] * jnp.exp(other[0:1] - highest)
    total = jnp.log(summed) + highest

    lane = lax.broadcasted_iota(jnp.int32, (1, LANES), 1)
    slot = jnp.where(lane < rows, stats[2:3], other[2:3]).astype(jnp.int32)
    live = slot >= 0
    slot = jnp.where(live & (lane >= rows), slot + rows, slot)
    live = jnp.concatenate([live, live], axis=1)
    weights = jnp.where(live, jnp.exp(scores - jnp.concatenate([total, total], axis=1)), 0.0).astype(BF16)
    sums_ref[...] = jnp.dot(weights, images_ref[...], preferred_element_type=F32)
    straight, swapped = [], []
    for b in range(len(block_of)):
        back = block_of[-1 - b]
        straight.append(sums_ref[0:half, block_of[b]] + rolled(sums_ref[2 * half:3 * half, back], BOX))
        swapped.append(sums_ref[half:2 * half, block_of[b]] + rolled(sums_ref[3 * half:, back], BOX))
    swapped = jnp.concatenate(swapped, axis=0)
    upper = swapped.astype(BF16)
    lower = (swapped - upper.astype(F32)).astype(BF16)
    mirror = mirror_of_rows()
    swapped = jnp.dot(upper, mirror, preferred_element_type=F32) + jnp.dot(
        lower, mirror, preferred_element_type=F32
    )
    for b in range(len(block_of)):
        both = straight[b] + swapped[b * half:(b + 1) * half]
        first_ref[:, block_of[b]] = both[:per_dev].astype(BF16)
        second_ref[:, block_of[b]] = both[per_dev:].astype(BF16)

    per_class = jnp.sum(weights.astype(F32), axis=1, keepdims=True)
    per_class = per_class[0:half] + per_class[half:2 * half] + per_class[2 * half:3 * half] + per_class[3 * half:]
    high, middle, low = three_parts(per_class)
    lanes = lax.broadcasted_iota(jnp.int32, (half, LANES), 1)
    sent = jnp.where(lanes == 0, high, jnp.where(lanes == 1, middle, jnp.where(lanes == 2, low, 0.0)))
    extra = slice(pixels, pixels + LANES)
    first_ref[:, extra] = sent[:per_dev].astype(BF16)
    second_ref[:, extra] = sent[per_dev:].astype(BF16)

    placing = (slot == lax.broadcasted_iota(jnp.int32, (LANES, LANES), 0)).astype(BF16)
    pieces = jnp.concatenate([*three_parts(total), jnp.zeros((5, LANES), F32)], axis=0)
    pieces = lax.dot_general(
        pieces.astype(BF16), placing, (((1,), (1,)), ((), ())), preferred_element_type=F32
    )
    total_ref[...] = pieces[0:1] + pieces[1:2] + pieces[2:3]
    last = slice(pixels + LANES, pixels + 2 * LANES)
    first_ref[:, last] = pieces[:per_dev].astype(BF16)
    second_ref[:, last] = jnp.zeros((per_dev, LANES), BF16)
    kept_ref[...] = first_ref[...]


def add_kernel(pd_ref, qx_ref, po_ref, qx1_ref, kept_ref, out_ref):
    pixels = out_ref.shape[1] - LANES
    own = jnp.where(leads(), kept_ref[:, :pixels].astype(F32), pd_ref[:, :pixels].astype(F32))
    out_ref[:, :pixels] = (qx_ref[:, :pixels].astype(F32) + qx1_ref[:, :pixels].astype(F32)) + (
        own + po_ref[:, :pixels].astype(F32)
    )
    pieces = po_ref[:, pixels:].astype(F32)
    out_ref[:, pixels:] = jnp.broadcast_to(pieces[0:1] + pieces[1:2] + pieces[2:3], (out_ref.shape[0], LANES))


def finish_kernel(own_ref, other_ref, total_ref, means_hbm, weights_hbm, loglik_hbm,
                  means_ref, weights_ref, loglik_ref, sent):
    per_dev, pixels = means_ref.shape
    capacity = loglik_ref.shape[1] // 2
    extra = slice(pixels, pixels + LANES)
    last = slice(pixels + LANES, pixels + 2 * LANES)
    pieces = sent.shape[0] - 2
    width = pixels // pieces
    count = own_ref[:, extra] + other_ref[:, extra]
    count = count[:, 0:1] + count[:, 1:2] + count[:, 2:3]
    divisor = count + 1.0
    copies = []
    for piece in range(pieces):
        span = pl.ds(piece * width, width)
        means_ref[:, span] = (own_ref[:, span] + other_ref[:, span]) / divisor
        copies.append(pltpu.make_async_copy(means_ref.at[:, span], means_hbm.at[:, span], sent.at[piece]))
        copies[-1].start()
    across = lax.broadcasted_iota(jnp.int32, (per_dev, per_dev), 1)
    down = lax.broadcasted_iota(jnp.int32, (per_dev, per_dev), 0)
    weights_ref[...] = jnp.sum(jnp.where(across == down, count, 0.0), axis=0, keepdims=True)
    copies.append(pltpu.make_async_copy(weights_ref, weights_hbm, sent.at[pieces]))
    copies[-1].start()
    first = lax.axis_index("img") == 0
    arrived = jnp.where(leads(), own_ref[0:1, last], rolled(other_ref[0:1, last], 2 * capacity))
    arrived = jnp.where(first, arrived[:, :capacity], arrived[:, capacity:2 * capacity])
    mine = jnp.where(first, total_ref[:, :capacity], total_ref[:, capacity:2 * capacity])
    loglik_ref[:, :capacity] = jnp.where(first, mine, arrived)
    loglik_ref[:, capacity:] = jnp.where(first, arrived, mine)
    copies.append(pltpu.make_async_copy(loglik_ref, loglik_hbm, sent.at[pieces + 1]))
    copies[-1].start()
    for copy in copies:
        copy.wait()


def passed_along(array, axis, by):
    devices = lax.axis_size(axis)
    return lax.ppermute(array, axis, [(i, (i + by) % devices) for i in range(devices)])


def turn_image(field, turn_index):
    square = field.reshape(field.shape[:-1] + (BOX, BOX))
    if turn_index >= 4:
        square = jnp.flip(square, -1)
    square = jnp.rot90(square, turn_index % 4, axes=(-2, -1))
    return square.reshape(field.shape)


def turn_back(field, turn_index):
    square = field.reshape(field.shape[:-1] + (BOX, BOX))
    square = jnp.rot90(square, -(turn_index % 4), axes=(-2, -1))
    if turn_index >= 4:
        square = jnp.flip(square, -1)
    return square.reshape(field.shape)


def slot_table(count_row, owner_row, read_rows, capacity):
    mic_count = count_row.shape[0]
    ends = jnp.cumsum(count_row)
    position = jnp.arange(read_rows, dtype=jnp.int32)
    micrograph = jnp.sum((position[:, None] >= ends[None, :]).astype(jnp.int32), axis=1)
    usable = position < ends[mic_count - 1]
    matches = micrograph[:, None] == jnp.arange(mic_count, dtype=jnp.int32)[None, :]
    target = jnp.sum(jnp.where(matches, owner_row[None, :], 0), axis=1)
    earlier = (
        (target[:, None] == target[None, :])
        & usable[None, :]
        & (position[None, :] < position[:, None])
    )
    ranking = jnp.sum(earlier.astype(jnp.int32), axis=1)
    slot_index = jnp.where(usable, target * capacity + ranking, -1)
    placing = slot_index[None, :] == jnp.arange(read_rows, dtype=jnp.int32)[:, None]
    return (usable, placing)


def class_scores(particle_rows, piece):
    pixels = piece.shape[1]
    turned = jnp.stack(
        [turn_image(piece, turn_index) for turn_index in range(ROTS)], axis=1
    ).reshape(-1, pixels)
    squares = jnp.sum(piece.astype(jnp.float32) ** 2, axis=1)
    inner = lax.dot_general(
        particle_rows, turned, (((1,), (1,)), ((), ())), preferred_element_type=jnp.float32
    )
    return inner - 0.5 * jnp.repeat(squares, ROTS)[None, :]


def class_block(weights, particle_rows, first_class, class_count):
    chosen = lax.dynamic_slice_in_dim(weights, first_class * ROTS, class_count * ROTS, 1)
    summed = lax.dot_general(
        chosen, particle_rows, (((0,), (0,)), ((), ())), preferred_element_type=jnp.float32
    )
    summed = summed.reshape(class_count, ROTS, summed.shape[1])
    result = turn_back(summed[:, 0], 0)
    for turn_index in range(1, ROTS):
        result = result + turn_back(summed[:, turn_index], turn_index)
    return result


def local(images, counts, owners, references):
    read_rows, pixels = images.shape
    n_img = lax.axis_size("img")
    n_cls = lax.axis_size("cls")
    capacity = read_rows // n_img
    per_dev = references.shape[0]
    classes = per_dev * n_cls
    usable, placing = slot_table(counts[0], owners[0], read_rows, capacity)
    packed = jnp.dot(
        placing.astype(jnp.bfloat16), images, preferred_element_type=jnp.float32
    ).astype(jnp.bfloat16)
    filled = jnp.sum(placing.astype(jnp.float32), axis=1).astype(jnp.bfloat16)
    moved, arrived = (
        lax.all_to_all(
            packed.reshape(n_img, capacity, pixels), "img", split_axis=0, concat_axis=0, tiled=True
        ),
        lax.all_to_all(
            filled.reshape(n_img, capacity), "img", split_axis=0, concat_axis=0, tiled=True
        ),
    )
    particle_rows = moved.reshape(read_rows, pixels)
    live_rows = arrived.reshape(read_rows) > 0
    scores = class_scores(particle_rows, lax.all_gather(references, "cls", axis=0, tiled=True))
    highest = jnp.max(scores, axis=1, keepdims=True)
    total = jnp.log(jnp.sum(jnp.exp(scores - highest), axis=1, keepdims=True)) + highest
    weights = jnp.where(live_rows[:, None], jnp.exp(scores - total), 0.0).astype(jnp.bfloat16)
    row_loglik = jnp.where(live_rows, total[:, 0], 0.0)
    column_sums = jnp.sum(
        jnp.sum(weights.astype(jnp.float32), axis=0).reshape(classes, ROTS), axis=1
    )
    totals = lax.psum(column_sums, ("cls", "img", "rd"))
    device_index = lax.axis_index("cls")
    own_totals = lax.dynamic_slice_in_dim(totals, device_index * per_dev, per_dev)

    def cycle_stop(stop_index, carried):
        block = (device_index - 1 - stop_index) % n_cls
        carried = carried + class_block(weights, particle_rows, block * per_dev, per_dev)
        return passed_along(carried, "cls", 1)

    carried = lax.fori_loop(0, n_cls - 1, cycle_stop, jnp.zeros((per_dev, pixels), jnp.float32))
    class_sums = carried + class_block(weights, particle_rows, device_index * per_dev, per_dev)
    class_sums = lax.psum(class_sums, ("img", "rd"))
    class_means = class_sums / (own_totals[:, None] + 1.0)
    return (class_means, own_totals, row_loglik)


def swapped(array):
    return lax.ppermute(array, "rd", [(0, 1), (1, 0)])


def traded(array, steps):
    pairs = []
    for source in range(16):
        role = (source & 1) ^ (source >> 2 in (1, 2))
        target = (source & ~1) ^ steps[role]
        pairs.append((source, target | (role ^ (target >> 2 in (1, 2)))))
    return lax.ppermute(array, LINKED, pairs)


def call(kernel, outs, args, scalars=(), scratch=(), in_hbm=(), outs_in_hbm=False):
    specs = [
        pl.BlockSpec(memory_space=pltpu.SMEM if i in scalars else pltpu.HBM if i in in_hbm else pltpu.VMEM)
        for i in range(len(args))
    ]
    out_space = pltpu.HBM if outs_in_hbm else pltpu.VMEM
    return pl.pallas_call(
        kernel,
        out_shape=outs,
        in_specs=specs,
        out_specs=jax.tree.map(lambda _: pl.BlockSpec(memory_space=out_space), outs),
        scratch_shapes=list(scratch),
        compiler_params=pltpu.CompilerParams(vmem_limit_bytes=16 * 1024 * 1024),
    )(*args)


def direct(images, counts, owners, references):
    read_rows, pixels = images.shape
    if 2 * read_rows != LANES:
        return local(images, counts, owners, references)
    capacity = read_rows // lax.axis_size("img")
    per_dev = references.shape[0]
    other_images = swapped(images)
    ref_one = traded(references, (4, 2))
    ref_two = traded(references, (8, 12))
    shape = jax.ShapeDtypeStruct
    in_hbm = [pltpu.with_memory_space_constraint(x, pltpu.HBM) for x in (images, counts, owners, references)]
    turned, flat, slots, classes = call(
        functools.partial(turn_kernel, capacity),
        (shape((pixels, 2 * LANES), BF16), shape((2 * LANES, pixels), BF16), shape((8, LANES), F32),
         shape(references.shape, BF16)),
        (*in_hbm, other_images), (),
        [pltpu.VMEM(counts.shape, jnp.int32),
         pltpu.VMEM(owners.shape, jnp.int32), pltpu.SemaphoreType.DMA((5,))],
        in_hbm=(0, 1, 2, 3),
    )
    scores, sent = call(
        score_kernel,
        (shape((8 * per_dev, 2 * LANES), F32), shape((4 * per_dev + 8, 2 * LANES), F32)),
        (slots, ref_two, ref_one, classes, turned), (),
        [pltpu.VMEM((8 * per_dev, pixels), BF16)],
    )
    arrived = swapped(sent)
    wide = pixels + 2 * LANES
    first, second, totals, kept = call(
        weigh_kernel,
        (shape((per_dev, wide), BF16), shape((per_dev, wide), BF16), shape((1, LANES), F32), shape((per_dev, wide), BF16)),
        (scores, sent, arrived, flat), (), [pltpu.VMEM((8 * per_dev, pixels), F32)],
    )
    po = traded(first, (2, 12))
    pd = traded(first, (2, 14))
    qx1 = traded(second, (10, 4))
    qx = traded(second, (8, 6))
    summed = call(add_kernel, shape((per_dev, wide), F32), (pd, qx, po, qx1, kept))
    other = swapped(summed)
    outs = (shape((per_dev, pixels), F32), shape((1, per_dev), F32), shape((1, read_rows), F32))
    means, weights, loglik = call(
        finish_kernel, outs, (summed, other, totals), (),
        [pltpu.VMEM(out.shape, out.dtype) for out in outs] + [pltpu.SemaphoreType.DMA((3,))],
        outs_in_hbm=True,
    )
    return means, weights.reshape(per_dev), loglik.reshape(read_rows)


def solution(mesh):
    sizes = mesh.shape
    small = sizes["cls"] == 4 and sizes["img"] == 2 and sizes["rd"] == 2
    placed = (
        P(("groups", "cls", "img", "rd"), None),
        P(("groups", "cls", "img", "rd"), None),
        P(("groups", "cls", "img", "rd"), None),
        P(("groups", "cls"), None),
    )
    return jax.shard_map(
        direct if small else local,
        mesh=mesh,
        in_specs=placed,
        out_specs=(
            P(("groups", "cls"), None),
            P(("groups", "cls")),
            P(("groups", "cls", "img", "rd")),
        ),
        check_vma=False,
    )
```

```python
import functools

import jax
import jax.numpy as jnp
from jax import lax
from jax.experimental import pallas as pl
from jax.experimental.pallas import tpu as pltpu
from jax.sharding import PartitionSpec as P

BOX = 64
ROTS = 8
LANES = 128
PAIR = LANES // BOX
LINKED = ("cls", "img", "rd")
F32 = jnp.float32
BF16 = jnp.bfloat16


def rolled(tile, by):
    if tile.shape[1] == LANES and by == BOX:
        return pltpu.roll(tile, BOX, 1)
    return jnp.concatenate([tile[:, by:], tile[:, :by]], axis=1)


def spans(pixels):
    return [slice(b * LANES, (b + 1) * LANES) for b in range(pixels // LANES)]


def slot_row(counts_ref, owners_ref, capacity):
    mic_count = counts_ref.shape[1]
    counts = [counts_ref[:, m:m + 1] for m in range(mic_count)]
    owners = [owners_ref[:, m:m + 1] for m in range(mic_count)]
    position = lax.broadcasted_iota(jnp.int32, (1, LANES), 1)
    slot = jnp.full((1, LANES), -1, jnp.int32)
    start = jnp.zeros((1, 1), jnp.int32)
    for mic in range(mic_count):
        before = jnp.zeros((1, 1), jnp.int32)
        for earlier in range(mic):
            before = before + jnp.where(owners[earlier] == owners[mic], counts[earlier], 0)
        stop = start + counts[mic]
        inside = (position >= start) & (position < stop)
        slot = jnp.where(inside, position + (owners[mic] * capacity + before - start), slot)
        start = stop
    return slot


def turn_kernel(capacity, own_hbm, counts_hbm, owners_hbm, classes_hbm, other_ref,
                out_ref, flat_ref, slots_ref, classes_ref, counts_ref, owners_ref, arrived):
    pixels = other_ref.shape[1]
    pieces = arrived.shape[0] - 3
    width = pixels // pieces
    copies = []
    for piece in range(pieces):
        span = pl.ds(piece * width, width)
        copies.append(pltpu.make_async_copy(own_hbm.at[:, span], flat_ref.at[pl.ds(0, other_ref.shape[0]), span], arrived.at[piece]))
        copies[-1].start()
    small = [
        pltpu.make_async_copy(source, target, arrived.at[pieces + i])
        for i, (source, target) in enumerate(
            ((counts_hbm, counts_ref), (owners_hbm, owners_ref), (classes_hbm, classes_ref))
        )
    ]
    for copy in small:
        copy.start()
    for block, span in enumerate(spans(pixels)):
        if block * LANES % width == 0:
            copies[block * LANES // width].wait()
        flat_ref[other_ref.shape[0]:LANES, span] = other_ref[:, span]
        tile = flat_ref[:LANES, span]
        out_ref[span, :LANES] = tile.T
    square = out_ref[:, :LANES].reshape(BOX, BOX, LANES)
    out_ref[:, LANES:] = jnp.swapaxes(square, 0, 1).reshape(pixels, LANES)
    for span in spans(pixels):
        flat_ref[LANES:, span] = out_ref[span, LANES:].T
    for copy in small:
        copy.wait()
    slot = slot_row(counts_ref, owners_ref, capacity).astype(F32)
    slots_ref[...] = jnp.broadcast_to(slot, slots_ref.shape)


def three_parts(value):
    high = value.astype(BF16).astype(F32)
    rest = value - high
    middle = rest.astype(BF16).astype(F32)
    return high, middle, (rest - middle).astype(BF16).astype(F32)


def leads():
    place = lax.axis_index("cls")
    inner = ((place == 1) | (place == 2)).astype(jnp.int32)
    return lax.axis_index("rd") == inner


def mirror_of_rows():
    row = lax.broadcasted_iota(jnp.int32, (LANES, LANES), 0)
    column = lax.broadcasted_iota(jnp.int32, (LANES, LANES), 1)
    return (column == (row // BOX) * BOX + (BOX - 1 - row % BOX)).astype(BF16)


def score_kernel(slots_ref, two_ref, one_ref, own_ref, images_ref, scores_ref, sent_ref,
                 flipped_ref):
    per_dev, pixels = own_ref.shape
    half = 2 * per_dev
    block_of = spans(pixels)
    swapped_block = jnp.where(leads(), one_ref[...].astype(F32), own_ref[...].astype(F32))
    refs = jnp.concatenate([two_ref[...].astype(F32), swapped_block], axis=0)
    squares = jnp.sum(refs * refs, axis=1, keepdims=True)
    stacked = jnp.concatenate([refs[:, b] for b in block_of], axis=0)
    mirrored = jnp.dot(stacked.astype(BF16), mirror_of_rows(), preferred_element_type=F32)
    for b in range(len(block_of)):
        part = slice(b * half, (b + 1) * half)
        both = jnp.concatenate([stacked[part], mirrored[part]], axis=0)
        flipped_ref[:2 * half, block_of[b]] = both.astype(BF16)
        flipped_ref[2 * half:, block_of[-1 - b]] = rolled(both, BOX).astype(BF16)
    inner = jnp.dot(flipped_ref[...], images_ref[...], preferred_element_type=F32)
    scores = inner - 0.5 * jnp.concatenate([squares] * 4, axis=0)
    scores_ref[...] = scores
    for f in range(4):
        sent_ref[f * per_dev:(f + 1) * per_dev] = scores[f * half + per_dev:(f + 1) * half]
    highest = jnp.max(scores, axis=0, keepdims=True)
    highest = jnp.maximum(highest[:, :LANES], highest[:, LANES:])
    summed = jnp.sum(jnp.exp(scores - jnp.concatenate([highest, highest], axis=1)), axis=0, keepdims=True)
    summed = summed[:, :LANES] + summed[:, LANES:]
    stats = jnp.concatenate([highest, summed, slots_ref[2:]], axis=0)
    sent_ref[4 * per_dev:] = jnp.concatenate([stats, stats], axis=1)


def weigh_kernel(scores_ref, sent_ref, arrived_ref, images_ref, first_ref, second_ref, total_ref, kept_ref, sums_ref):
    per_dev = first_ref.shape[0]
    pixels = images_ref.shape[1]
    rows = LANES // 2
    half = 2 * per_dev
    block_of = spans(pixels)
    top = 4 * per_dev
    stats = sent_ref[top:, :LANES]
    other = rolled(arrived_ref[top:, :LANES], BOX)
    arrived = jnp.concatenate(
        [rolled(arrived_ref[:top, :LANES], BOX), rolled(arrived_ref[:top, LANES:], BOX)], axis=1
    )
    lead = leads()
    scores = []
    for f in range(4):
        here, there = scores_ref[f * half:f * half + per_dev], arrived[f * per_dev:(f + 1) * per_dev]
        scores += [jnp.where(lead, there, here), jnp.where(lead, here, there)]
    scores = jnp.concatenate(scores, axis=0)
    highest = jnp.maximum(stats[0:1], other[0:1])
    summed = stats[1:2] * jnp.exp(stats[0:1] - highest) + other[1:2] * jnp.exp(other[0:1] - highest)
    total = jnp.log(summed) + highest

    lane = lax.broadcasted_iota(jnp.int32, (1, LANES), 1)
    slot = jnp.where(lane < rows, stats[2:3], other[2:3]).astype(jnp.int32)
    live = slot >= 0
    slot = jnp.where(live & (lane >= rows), slot + rows, slot)
    live = jnp.concatenate([live, live], axis=1)
    weights = jnp.where(live, jnp.exp(scores - jnp.concatenate([total, total], axis=1)), 0.0).astype(BF16)
    sums_ref[...] = jnp.dot(weights, images_ref[...], preferred_element_type=F32)
    straight, swapped = [], []
    for b in range(len(block_of)):
        back = block_of[-1 - b]
        straight.append(sums_ref[0:half, block_of[b]] + rolled(sums_ref[2 * half:3 * half, back], BOX))
        swapped.append(sums_ref[half:2 * half, block_of[b]] + rolled(sums_ref[3 * half:, back], BOX))
    swapped = jnp.concatenate(swapped, axis=0)
    upper = swapped.astype(BF16)
    lower = (swapped - upper.astype(F32)).astype(BF16)
    mirror = mirror_of_rows()
    swapped = jnp.dot(upper, mirror, preferred_element_type=F32) + jnp.dot(
        lower, mirror, preferred_element_type=F32
    )
    for b in range(len(block_of)):
        both = straight[b] + swapped[b * half:(b + 1) * half]
        first_ref[:, block_of[b]] = both[:per_dev].astype(BF16)
        second_ref[:, block_of[b]] = both[per_dev:].astype(BF16)

    per_class = jnp.sum(weights.astype(F32), axis=1, keepdims=True)
    per_class = per_class[0:half] + per_class[half:2 * half] + per_class[2 * half:3 * half] + per_class[3 * half:]
    high, middle, low = three_parts(per_class)
    lanes = lax.broadcasted_iota(jnp.int32, (half, LANES), 1)
    sent = jnp.where(lanes == 0, high, jnp.where(lanes == 1, middle, jnp.where(lanes == 2, low, 0.0)))
    extra = slice(pixels, pixels + LANES)
    first_ref[:, extra] = sent[:per_dev].astype(BF16)
    second_ref[:, extra] = sent[per_dev:].astype(BF16)

    placing = (slot == lax.broadcasted_iota(jnp.int32, (LANES, LANES), 0)).astype(BF16)
    pieces = jnp.concatenate([*three_parts(total), jnp.zeros((5, LANES), F32)], axis=0)
    pieces = lax.dot_general(
        pieces.astype(BF16), placing, (((1,), (1,)), ((), ())), preferred_element_type=F32
    )
    total_ref[...] = pieces[0:1] + pieces[1:2] + pieces[2:3]
    last = slice(pixels + LANES, pixels + 2 * LANES)
    first_ref[:, last] = pieces[:per_dev].astype(BF16)
    second_ref[:, last] = jnp.zeros((per_dev, LANES), BF16)
    kept_ref[...] = first_ref[...]


def add_kernel(po_ref, qx_ref, pd_ref, qx1_ref, kept_ref, out_ref):
    pixels = out_ref.shape[1] - LANES
    own = jnp.where(leads(), kept_ref[:, :pixels].astype(F32), pd_ref[:, :pixels].astype(F32))
    out_ref[:, :pixels] = (qx_ref[:, :pixels].astype(F32) + qx1_ref[:, :pixels].astype(F32)) + (
        own + po_ref[:, :pixels].astype(F32)
    )
    pieces = po_ref[:, pixels:].astype(F32)
    out_ref[:, pixels:] = jnp.broadcast_to(pieces[0:1] + pieces[1:2] + pieces[2:3], (out_ref.shape[0], LANES))


def finish_kernel(own_ref, other_ref, total_ref, means_hbm, weights_hbm, loglik_hbm,
                  means_ref, weights_ref, loglik_ref, sent):
    per_dev, pixels = means_ref.shape
    capacity = loglik_ref.shape[1] // 2
    extra = slice(pixels, pixels + LANES)
    last = slice(pixels + LANES, pixels + 2 * LANES)
    pieces = sent.shape[0] - 2
    width = pixels // pieces
    count = own_ref[:, extra] + other_ref[:, extra]
    count = count[:, 0:1] + count[:, 1:2] + count[:, 2:3]
    divisor = count + 1.0
    copies = []
    for piece in range(pieces):
        span = pl.ds(piece * width, width)
        means_ref[:, span] = (own_ref[:, span] + other_ref[:, span]) / divisor
        copies.append(pltpu.make_async_copy(means_ref.at[:, span], means_hbm.at[:, span], sent.at[piece]))
        copies[-1].start()
    across = lax.broadcasted_iota(jnp.int32, (per_dev, per_dev), 1)
    down = lax.broadcasted_iota(jnp.int32, (per_dev, per_dev), 0)
    weights_ref[...] = jnp.sum(jnp.where(across == down, count, 0.0), axis=0, keepdims=True)
    copies.append(pltpu.make_async_copy(weights_ref, weights_hbm, sent.at[pieces]))
    copies[-1].start()
    first = lax.axis_index("img") == 0
    arrived = jnp.where(leads(), own_ref[0:1, last], rolled(other_ref[0:1, last], 2 * capacity))
    arrived = jnp.where(first, arrived[:, :capacity], arrived[:, capacity:2 * capacity])
    mine = jnp.where(first, total_ref[:, :capacity], total_ref[:, capacity:2 * capacity])
    loglik_ref[:, :capacity] = jnp.where(first, mine, arrived)
    loglik_ref[:, capacity:] = jnp.where(first, arrived, mine)
    copies.append(pltpu.make_async_copy(loglik_ref, loglik_hbm, sent.at[pieces + 1]))
    copies[-1].start()
    for copy in copies:
        copy.wait()


def passed_along(array, axis, by):
    devices = lax.axis_size(axis)
    return lax.ppermute(array, axis, [(i, (i + by) % devices) for i in range(devices)])


def turn_image(field, turn_index):
    square = field.reshape(field.shape[:-1] + (BOX, BOX))
    if turn_index >= 4:
        square = jnp.flip(square, -1)
    square = jnp.rot90(square, turn_index % 4, axes=(-2, -1))
    return square.reshape(field.shape)


def turn_back(field, turn_index):
    square = field.reshape(field.shape[:-1] + (BOX, BOX))
    square = jnp.rot90(square, -(turn_index % 4), axes=(-2, -1))
    if turn_index >= 4:
        square = jnp.flip(square, -1)
    return square.reshape(field.shape)


def slot_table(count_row, owner_row, read_rows, capacity):
    mic_count = count_row.shape[0]
    ends = jnp.cumsum(count_row)
    position = jnp.arange(read_rows, dtype=jnp.int32)
    micrograph = jnp.sum((position[:, None] >= ends[None, :]).astype(jnp.int32), axis=1)
    usable = position < ends[mic_count - 1]
    matches = micrograph[:, None] == jnp.arange(mic_count, dtype=jnp.int32)[None, :]
    target = jnp.sum(jnp.where(matches, owner_row[None, :], 0), axis=1)
    earlier = (
        (target[:, None] == target[None, :])
        & usable[None, :]
        & (position[None, :] < position[:, None])
    )
    ranking = jnp.sum(earlier.astype(jnp.int32), axis=1)
    slot_index = jnp.where(usable, target * capacity + ranking, -1)
    placing = slot_index[None, :] == jnp.arange(read_rows, dtype=jnp.int32)[:, None]
    return (usable, placing)


def class_scores(particle_rows, piece):
    pixels = piece.shape[1]
    turned = jnp.stack(
        [turn_image(piece, turn_index) for turn_index in range(ROTS)], axis=1
    ).reshape(-1, pixels)
    squares = jnp.sum(piece.astype(jnp.float32) ** 2, axis=1)
    inner = lax.dot_general(
        particle_rows, turned, (((1,), (1,)), ((), ())), preferred_element_type=jnp.float32
    )
    return inner - 0.5 * jnp.repeat(squares, ROTS)[None, :]


def class_block(weights, particle_rows, first_class, class_count):
    chosen = lax.dynamic_slice_in_dim(weights, first_class * ROTS, class_count * ROTS, 1)
    summed = lax.dot_general(
        chosen, particle_rows, (((0,), (0,)), ((), ())), preferred_element_type=jnp.float32
    )
    summed = summed.reshape(class_count, ROTS, summed.shape[1])
    result = turn_back(summed[:, 0], 0)
    for turn_index in range(1, ROTS):
        result = result + turn_back(summed[:, turn_index], turn_index)
    return result


def local(images, counts, owners, references):
    read_rows, pixels = images.shape
    n_img = lax.axis_size("img")
    n_cls = lax.axis_size("cls")
    capacity = read_rows // n_img
    per_dev = references.shape[0]
    classes = per_dev * n_cls
    usable, placing = slot_table(counts[0], owners[0], read_rows, capacity)
    packed = jnp.dot(
        placing.astype(jnp.bfloat16), images, preferred_element_type=jnp.float32
    ).astype(jnp.bfloat16)
    filled = jnp.sum(placing.astype(jnp.float32), axis=1).astype(jnp.bfloat16)
    moved, arrived = (
        lax.all_to_all(
            packed.reshape(n_img, capacity, pixels), "img", split_axis=0, concat_axis=0, tiled=True
        ),
        lax.all_to_all(
            filled.reshape(n_img, capacity), "img", split_axis=0, concat_axis=0, tiled=True
        ),
    )
    particle_rows = moved.reshape(read_rows, pixels)
    live_rows = arrived.reshape(read_rows) > 0
    scores = class_scores(particle_rows, lax.all_gather(references, "cls", axis=0, tiled=True))
    highest = jnp.max(scores, axis=1, keepdims=True)
    total = jnp.log(jnp.sum(jnp.exp(scores - highest), axis=1, keepdims=True)) + highest
    weights = jnp.where(live_rows[:, None], jnp.exp(scores - total), 0.0).astype(jnp.bfloat16)
    row_loglik = jnp.where(live_rows, total[:, 0], 0.0)
    column_sums = jnp.sum(
        jnp.sum(weights.astype(jnp.float32), axis=0).reshape(classes, ROTS), axis=1
    )
    totals = lax.psum(column_sums, ("cls", "img", "rd"))
    device_index = lax.axis_index("cls")
    own_totals = lax.dynamic_slice_in_dim(totals, device_index * per_dev, per_dev)

    def cycle_stop(stop_index, carried):
        block = (device_index - 1 - stop_index) % n_cls
        carried = carried + class_block(weights, particle_rows, block * per_dev, per_dev)
        return passed_along(carried, "cls", 1)

    carried = lax.fori_loop(0, n_cls - 1, cycle_stop, jnp.zeros((per_dev, pixels), jnp.float32))
    class_sums = carried + class_block(weights, particle_rows, device_index * per_dev, per_dev)
    class_sums = lax.psum(class_sums, ("img", "rd"))
    class_means = class_sums / (own_totals[:, None] + 1.0)
    return (class_means, own_totals, row_loglik)


def swapped(array):
    return lax.ppermute(array, "rd", [(0, 1), (1, 0)])


def traded(array, steps):
    pairs = []
    for source in range(16):
        role = (source & 1) ^ (source >> 2 in (1, 2))
        target = (source & ~1) ^ steps[role]
        pairs.append((source, target | (role ^ (target >> 2 in (1, 2)))))
    return lax.ppermute(array, LINKED, pairs)


def call(kernel, outs, args, scalars=(), scratch=(), in_hbm=(), outs_in_hbm=False):
    specs = [
        pl.BlockSpec(memory_space=pltpu.SMEM if i in scalars else pltpu.HBM if i in in_hbm else pltpu.VMEM)
        for i in range(len(args))
    ]
    out_space = pltpu.HBM if outs_in_hbm else pltpu.VMEM
    return pl.pallas_call(
        kernel,
        out_shape=outs,
        in_specs=specs,
        out_specs=jax.tree.map(lambda _: pl.BlockSpec(memory_space=out_space), outs),
        scratch_shapes=list(scratch),
        compiler_params=pltpu.CompilerParams(vmem_limit_bytes=16 * 1024 * 1024),
    )(*args)


def direct(images, counts, owners, references):
    read_rows, pixels = images.shape
    if 2 * read_rows != LANES:
        return local(images, counts, owners, references)
    capacity = read_rows // lax.axis_size("img")
    per_dev = references.shape[0]
    other_images = swapped(images)
    ref_one = traded(references, (4, 2))
    ref_two = traded(references, (8, 12))
    shape = jax.ShapeDtypeStruct
    in_hbm = [pltpu.with_memory_space_constraint(x, pltpu.HBM) for x in (images, counts, owners, references)]
    turned, flat, slots, classes = call(
        functools.partial(turn_kernel, capacity),
        (shape((pixels, 2 * LANES), BF16), shape((2 * LANES, pixels), BF16), shape((8, LANES), F32),
         shape(references.shape, BF16)),
        (*in_hbm, other_images), (),
        [pltpu.VMEM(counts.shape, jnp.int32),
         pltpu.VMEM(owners.shape, jnp.int32), pltpu.SemaphoreType.DMA((5,))],
        in_hbm=(0, 1, 2, 3),
    )
    scores, sent = call(
        score_kernel,
        (shape((8 * per_dev, 2 * LANES), F32), shape((4 * per_dev + 8, 2 * LANES), F32)),
        (slots, ref_two, ref_one, classes, turned), (),
        [pltpu.VMEM((8 * per_dev, pixels), BF16)],
    )
    arrived = swapped(sent)
    wide = pixels + 2 * LANES
    first, second, totals, kept = call(
        weigh_kernel,
        (shape((per_dev, wide), BF16), shape((per_dev, wide), BF16), shape((1, LANES), F32), shape((per_dev, wide), BF16)),
        (scores, sent, arrived, flat), (), [pltpu.VMEM((8 * per_dev, pixels), F32)],
    )
    po = traded(first, (2, 12))
    pd = traded(first, (2, 14))
    qx1 = traded(second, (10, 4))
    qx = traded(second, (8, 6))
    summed = call(add_kernel, shape((per_dev, wide), F32), (po, qx, pd, qx1, kept))
    other = swapped(summed)
    outs = (shape((per_dev, pixels), F32), shape((1, per_dev), F32), shape((1, read_rows), F32))
    means, weights, loglik = call(
        finish_kernel, outs, (summed, other, totals), (),
        [pltpu.VMEM(out.shape, out.dtype) for out in outs] + [pltpu.SemaphoreType.DMA((3,))],
        outs_in_hbm=True,
    )
    return means, weights.reshape(per_dev), loglik.reshape(read_rows)


def solution(mesh):
    sizes = mesh.shape
    small = sizes["cls"] == 4 and sizes["img"] == 2 and sizes["rd"] == 2
    placed = (
        P(("groups", "cls", "img", "rd"), None),
        P(("groups", "cls", "img", "rd"), None),
        P(("groups", "cls", "img", "rd"), None),
        P(("groups", "cls"), None),
    )
    return jax.shard_map(
        direct if small else local,
        mesh=mesh,
        in_specs=placed,
        out_specs=(
            P(("groups", "cls"), None),
            P(("groups", "cls")),
            P(("groups", "cls", "img", "rd")),
        ),
        check_vma=False,
    )
```
